256 devices in a mesh: blk: 32 (over y, x, z_lo), grp: 8 (over z_hi, core).
Axes of the slice: x: 4, y: 4, z: 8 (z_hi: 4, z_lo: 2; z = z_hi * 2 + z_lo), core: 2. Of those that a mesh axis runs over, the one named last changes fastest.
Arguments:
- patch_input: bfloat16 [131072, 1536], P(('blk', 'grp')), may hold values from -6 to 6
- hidden_pre: bfloat16 [73728, 3072], P(('blk', 'grp')), may hold values from -6 to 6
- down_weight: bfloat16 [3072, 1536], replicated, may hold values from -0.109375 to 0.109375
- text_features: bfloat16 [4096, 1536], P(('blk', 'grp')), may hold values from -6 to 6
- patch_counts: int32 [4096], P(('blk', 'grp')), may hold values from 1 to 497, as said below
- owners: int32 [131072], P(('blk', 'grp')), may hold values from -1 to 31, as said below
- pair_labels: int32 [4096], P(('blk', 'grp')), may hold values from 0 to 4095, as said below
Outputs:
- d_patches: bfloat16 [131072, 1536], P(('blk', 'grp'))
- d_hidden: bfloat16 [73728, 3072], P(('blk', 'grp'))
The draws below stay inside these ranges and needn't reach their ends.
Inputs may be any that keep to these rules, and one draw needn't show every extreme that they name: `patch_counts`: each block of 512 patch slots holds 16 images; their counts sum to the block's live slots, which are the block's first slots; at least 64 are live, and in each grp index some block has all 512 live. Some image has exactly 497 patches. owners is -1 exactly on the slots that no image takes. Among the blocks of one grp index, every blk index is named by exactly 288 live slots; one block names one blk index at most 17 times, exactly 17 in some block of each grp index. `pair_labels`: the paired text of image i lies in a group 0 to 3 groups before image i's group, cyclically over 32 groups.
All inputs are finite; a program needn't handle non-finite values.
Results may differ from the reference program's by a relative error of at most 0.0065.
Values may be sent and summed in bfloat16 or wider, within the bound.
No kernel may reach another device: no remote copies, remote signals or barrier semaphores. Data moves between devices by JAX's collectives and lax.ppermute only.
A program may use at most 128 MiB of HBM per device.

```python
import jax
import jax.numpy as jnp
from jax import lax

D = 1536
FF = 3072
IMG_DEV = 16
SLOTS = 512
STEPS = 4
BAL = 288
IMAGES = 4096
PATCH_SLOTS = 131072
HIDDEN_ROWS = 73728
N_BLK = 32
N_GRP = 8


def patch_layout(key):
    base_key = jax.random.fold_in(key, 11)
    subkeys = jax.random.split(base_key, 4)
    top_load = SLOTS // N_BLK - 2
    halves = N_BLK // 2
    positions = jnp.arange(N_BLK, dtype=jnp.int32)
    shares = 1 + (positions >= N_BLK // 4).astype(jnp.int32) + (positions >= 3 * N_BLK // 4).astype(jnp.int32)
    low_part = jnp.arange(halves, dtype=jnp.int32) * top_load // max(halves - 1, 1)
    load_values = jnp.concatenate([low_part, top_load - low_part]).astype(jnp.int32)
    share_perm = jax.vmap(lambda subkey: jax.random.permutation(subkey, shares))(jax.random.split(subkeys[0], N_GRP))
    load_perm = jax.vmap(lambda subkey: jax.random.permutation(subkey, load_values))(jax.random.split(subkeys[1], N_GRP))
    offset_index = (positions[None, :] - positions[:, None]) % N_BLK
    matrix = share_perm[:, offset_index] + load_perm[:, :, None]
    matrix = jnp.transpose(matrix, (1, 0, 2))
    cumulative = jnp.cumsum(matrix, axis=-1)
    live_count = cumulative[..., -1]
    slot_ids = jnp.arange(SLOTS, dtype=jnp.int32)
    base_owner = jnp.sum((cumulative[:, :, None, :] <= slot_ids[None, None, :, None]).astype(jnp.int32), axis=-1)
    is_live = slot_ids[None, None, :] < live_count[:, :, None]
    scores = jax.random.randint(subkeys[2], (N_BLK, N_GRP, SLOTS), 0, 2 ** 20) * SLOTS + slot_ids
    scores = jnp.where(is_live, scores, 2 ** 30 + slot_ids)
    ordering = jnp.argsort(scores, axis=-1, stable=True)
    permuted = jnp.take_along_axis(base_owner, ordering, axis=-1)
    owner_table = jnp.where(is_live, permuted, -1).astype(jnp.int32)
    extra_count = live_count - IMG_DEV
    image_picks = jax.random.randint(subkeys[3], (N_BLK, N_GRP, SLOTS), 0, IMG_DEV)
    used = slot_ids[None, None, :] < extra_count[:, :, None]
    image_ids = jnp.arange(IMG_DEV, dtype=jnp.int32)
    hits = (image_picks[..., None] == image_ids) & used[..., None]
    counts = 1 + jnp.sum(hits.astype(jnp.int32), axis=2)
    is_full = live_count == SLOTS
    chosen = (image_picks[:, :, 0][..., None] == image_ids).astype(jnp.int32)
    full_counts = 1 + extra_count[..., None] * chosen
    counts = jnp.where(is_full[..., None], full_counts, counts)
    return (counts.reshape(-1).astype(jnp.int32), owner_table.reshape(-1))


def draw_patch_counts(key, part):
    return patch_layout(key)[0]


def draw_owners(key, part):
    return patch_layout(key)[1]


def draw_pair_labels(key, part):
    key = jax.random.fold_in(key, 7)
    subkeys = jax.random.split(key, 2)
    group_rows = N_GRP * IMG_DEV
    total = IMG_DEV * N_BLK * N_GRP
    own_block = jnp.arange(total, dtype=jnp.int32) // group_rows
    back_steps = jax.random.randint(subkeys[0], (total,), 0, STEPS)
    within = jax.random.randint(subkeys[1], (total,), 0, group_rows)
    return ((own_block - back_steps) % N_BLK * group_rows + within).astype(jnp.int32)


def steps_of(own_key, dims, cuts, smallest, top_value):
    def one(axis_at, parts):
        draws = jax.random.uniform(jax.random.fold_in(jax.random.fold_in(own_key, 6), axis_at), (parts,), jnp.float32, smallest / len(cuts), top_value / len(cuts))
        return jnp.repeat(jnp.exp(draws), dims[axis_at] // parts).reshape((-1,) + (1,) * (len(dims) - axis_at - 1))

    loudness = one(*cuts[0])
    for cut in cuts[1:]:
        loudness = loudness * one(*cut)
    return loudness


def scatter_about(own_key, dims, scale, most, cuts=(), kind=jnp.bfloat16):
    level = steps_of(own_key, dims, cuts, -0.22, 0.18) if cuts else 1.0
    result = jax.random.normal(own_key, dims, jnp.float32) * scale * level
    return jnp.minimum(jnp.maximum(result, -most), most).astype(kind)


def setup_inputs(seed: int = 0) -> dict:
    streams_of = jax.random.split(jax.random.key(seed), 8)
    return {
        "patch_input": scatter_about(streams_of[0], (PATCH_SLOTS, D), 1.0, 6.0, ((0, 256),)),
        "hidden_pre": scatter_about(streams_of[1], (HIDDEN_ROWS, FF), 1.0, 6.0, ((0, 256),)),
        "down_weight": scatter_about(streams_of[2], (FF, D), FF ** -0.5, 0.109375),
        "text_features": scatter_about(streams_of[3], (IMAGES, D), 1.0, 6.0, ((0, 256),)),
        "patch_counts": draw_patch_counts(jax.random.fold_in(streams_of[7], 71), 0),
        "owners": draw_owners(jax.random.fold_in(streams_of[7], 71), 0),
        "pair_labels": draw_pair_labels(jax.random.fold_in(streams_of[7], 71), 0),
    }


GELU_A = 0.7978845608028654
GELU_B = 0.044715
LOGIT_SCALE_TEMP = 10.0
LOGIT_BIAS_SHIFT = -2.0
LOSS_SCALE_FACTOR = 128.0

def gelu_tanh(entries):
    inside = GELU_A * (entries + GELU_B * entries * entries * entries)
    return 0.5 * entries * (1.0 + jnp.tanh(inside))

def gelu_slope(entries):
    inside = GELU_A * (entries + GELU_B * entries * entries * entries)
    tangent = jnp.tanh(inside)
    return 0.5 * (1.0 + tangent) + 0.5 * entries * (1.0 - tangent * tangent) * GELU_A * (1.0 + 3.0 * GELU_B * entries * entries)

def reference(patch_input, hidden_pre, down_weight, text_features, patch_counts, owners, pair_labels):
    blocks = N_BLK * N_GRP
    group_rows = N_GRP * IMG_DEV
    routing = owners.reshape(N_BLK, N_GRP, SLOTS)
    owner_hits = (routing[..., None] == jnp.arange(N_BLK, dtype=jnp.int32)).astype(jnp.int32)
    owner_rank = lax.optimization_barrier(jnp.sum((jnp.cumsum(owner_hits, axis=2) - 1) * owner_hits, axis=-1))
    tallies = lax.optimization_barrier(jnp.sum(owner_hits, axis=2))
    before = jnp.cumsum(tallies, axis=0) - tallies
    offsets = lax.optimization_barrier(jnp.sum(owner_hits * before[:, :, None, :], axis=-1))
    grp_ids = jnp.arange(N_GRP, dtype=jnp.int32)[None, :, None]
    target = (routing * N_GRP + grp_ids) * BAL + offsets + owner_rank
    is_live = routing >= 0
    target = jnp.where(is_live, target, blocks * BAL).reshape(-1).astype(jnp.int32)
    hidden_rows = jnp.take(hidden_pre, target, axis=0, mode='fill', fill_value=0)
    active = gelu_tanh(hidden_rows.astype(jnp.float32)).astype(jnp.bfloat16)
    branch = jnp.dot(active, down_weight, preferred_element_type=jnp.float32)
    summed = patch_input.astype(jnp.float32) + branch
    centered = summed - lax.optimization_barrier(jnp.mean(summed, axis=-1, keepdims=True))
    scale_inv = lax.rsqrt(lax.optimization_barrier(jnp.mean(centered * centered, axis=-1, keepdims=True)) + 1e-06)
    normed = centered * scale_inv
    counts = patch_counts.reshape(blocks, IMG_DEV)
    image_ends = jnp.cumsum(counts, axis=1)
    slot_ids = jnp.arange(SLOTS, dtype=jnp.int32)
    image_of = lax.optimization_barrier(jnp.sum((slot_ids[None, :, None] >= image_ends[:, None, :]).astype(jnp.int32), axis=-1))
    member = (image_of[:, None, :] == jnp.arange(IMG_DEV, dtype=jnp.int32)[None, :, None]).astype(jnp.float32)
    normed_blocks = normed.reshape(blocks, SLOTS, D)
    image_sizes = counts.astype(jnp.float32)[..., None]
    pooled = jnp.einsum('nis,nsd->nid', member, normed_blocks, precision=lax.Precision.HIGHEST) / image_sizes
    embed_norm = jnp.sqrt(lax.optimization_barrier(jnp.sum(pooled * pooled, axis=-1, keepdims=True)) + 1e-06)
    embedding = pooled / embed_norm
    image_embedding_final = embedding.astype(jnp.bfloat16).astype(jnp.float32).reshape(N_BLK, group_rows, D)
    text = text_features.astype(jnp.float32)
    text_b = (text / jnp.sqrt(lax.optimization_barrier(jnp.sum(text * text, axis=-1, keepdims=True)) + 1e-06)).astype(jnp.bfloat16)
    text_b = text_b.reshape(N_BLK, group_rows, D)
    labels = pair_labels.reshape(N_BLK, group_rows)
    columns = jnp.arange(group_rows, dtype=jnp.int32)
    embed_grad = jnp.zeros((N_BLK, group_rows, D), jnp.float32)
    for rotation in range(STEPS):
        current_text_block = jnp.roll(text_b, rotation, axis=0).astype(jnp.float32)
        source = (jnp.arange(N_BLK, dtype=jnp.int32) - rotation) % N_BLK
        pair_scores_matrix = LOGIT_SCALE_TEMP * jnp.einsum('yoa,yka->yok', image_embedding_final, current_text_block) + LOGIT_BIAS_SHIFT
        positive_mask = (labels[:, :, None] == source[:, None, None] * group_rows + columns[None, None, :]).astype(jnp.float32)
        pair_weight_matrix = (LOSS_SCALE_FACTOR * LOGIT_SCALE_TEMP * (jax.nn.sigmoid(pair_scores_matrix) - positive_mask)).astype(jnp.bfloat16)
        embed_grad = embed_grad + jnp.einsum('bij,bjd->bid', pair_weight_matrix.astype(jnp.float32), current_text_block)
    embed_grad = embed_grad.reshape(blocks, IMG_DEV, D)
    radial = lax.optimization_barrier(jnp.sum(embedding * embed_grad, axis=-1, keepdims=True))
    pooled_grad = (embed_grad - embedding * radial) / embed_norm
    spread = pooled_grad / image_sizes
    normed_grad = jnp.einsum('nis,nid->nsd', member, spread, precision=lax.Precision.HIGHEST).reshape(-1, D)
    mean_grad = lax.optimization_barrier(jnp.mean(normed_grad, axis=-1, keepdims=True))
    mean_cross = lax.optimization_barrier(jnp.mean(normed_grad * normed, axis=-1, keepdims=True))
    summed_grad = (normed_grad - mean_grad - normed * mean_cross) * scale_inv
    d_patches = summed_grad.astype(jnp.bfloat16)
    active_grad = lax.dot_general(d_patches, down_weight, (((1,), (1,)), ((), ())), preferred_element_type=jnp.float32)
    slot_grad = (gelu_slope(hidden_rows.astype(jnp.float32)) * active_grad).astype(jnp.bfloat16)
    d_hidden = jnp.zeros((blocks * BAL, FF), jnp.bfloat16).at[target].set(slot_grad, mode='drop')
    return (d_patches, d_hidden)
```

```python
import jax
import jax.numpy as jnp
from jax import lax
from jax.experimental import pallas as pl
from jax.experimental.pallas import tpu as pltpu
from jax.sharding import PartitionSpec as P

STEPS = 4
GELU_A = 0.7978845608028654
GELU_B = 0.044715
LOGIT_SCALE_TEMP = 10.0
LOGIT_BIAS_SHIFT = -2.0
LOSS_SCALE_FACTOR = 128.0

BLK = 32
CAP = 16
D = 1536
FF = 3072
SLOTS = 512
ROWS = 288
IMAGES = 16
LANES = 128
TILES = D // LANES
MSG = (TILES + 1) * CAP
WIDE = BLK * CAP
SLOT_K = 640
F32 = jnp.float32
BF16 = jnp.bfloat16
I32 = jnp.int32


def iota(shape, axis):
    return lax.broadcasted_iota(I32, shape, axis)


def vmem(count):
    return [pl.BlockSpec(memory_space=pltpu.VMEM)] * count


def params(mib):
    return pltpu.CompilerParams(vmem_limit_bytes=mib * 2**20)


def forward_kernel(hidden_ref, weight_ref, branch_ref, total):
    step = pl.program_id(0)
    entries = hidden_ref[...].astype(F32)
    inside = GELU_A * (entries + GELU_B * entries * entries * entries)
    active = (0.5 * entries * (1.0 + jnp.tanh(inside))).astype(BF16)
    part = jnp.dot(active, weight_ref[...], preferred_element_type=F32)

    @pl.when(step == 0)
    def _():
        total[...] = part

    @pl.when(step > 0)
    def _():
        total[...] += part

    @pl.when(step == pl.num_programs(0) - 1)
    def _():
        branch_ref[...] = total[...].astype(BF16)


def forward(hidden, weight):
    chunk = 512
    return pl.pallas_call(
        forward_kernel,
        grid=(FF // chunk,),
        in_specs=[
            pl.BlockSpec((ROWS, chunk), lambda k: (0, k)),
            pl.BlockSpec((chunk, D), lambda k: (k, 0)),
        ],
        out_specs=pl.BlockSpec((ROWS, D), lambda k: (0, 0)),
        out_shape=jax.ShapeDtypeStruct((ROWS, D), BF16),
        scratch_shapes=[pltpu.VMEM((ROWS, D), F32)],
        compiler_params=params(24),
        cost_estimate=pl.CostEstimate(
            flops=2 * ROWS * FF * D, bytes_accessed=2 * (FF * D + ROWS * FF), transcendentals=ROWS * FF
        ),
        name="owner_forward",
    )(hidden, weight)


def put_message(send_ref, wide, extra):
    for tile in range(TILES):
        send_ref[:, tile * CAP : (tile + 1) * CAP, :] = wide[
            :, tile * LANES : (tile + 1) * LANES
        ].reshape(BLK, CAP, LANES)
    stacked = jnp.concatenate(
        [extra[:, tile * LANES : (tile + 1) * LANES] for tile in range(TILES)], axis=0
    )
    row = iota((WIDE, TILES * BLK), 0)
    column = iota((WIDE, TILES * BLK), 1)
    pick = ((row >> 4) == (column & 31)) & ((row & 15) == (column >> 5))
    last = jnp.dot(pick.astype(F32).astype(BF16), stacked, preferred_element_type=F32)
    send_ref[:, TILES * CAP :, :] = last.astype(BF16).reshape(BLK, CAP, LANES)


def take_message(arrived_ref, rows_ref):
    for tile in range(TILES):
        rows_ref[0:WIDE, tile * LANES : (tile + 1) * LANES] = arrived_ref[
            :, tile * CAP : (tile + 1) * CAP, :
        ].reshape(WIDE, LANES)
    last = arrived_ref[:, TILES * CAP :, :].reshape(WIDE, LANES)
    row = iota((TILES * BLK, WIDE), 0)
    column = iota((TILES * BLK, WIDE), 1)
    pick = ((column >> 4) == (row & 31)) & ((column & 15) == (row >> 5))
    stacked = jnp.dot(pick.astype(F32).astype(BF16), last, preferred_element_type=F32).astype(BF16)
    for tile in range(TILES):
        rows_ref[WIDE : WIDE + BLK, tile * LANES : (tile + 1) * LANES] = stacked[
            tile * BLK : (tile + 1) * BLK, :
        ]
    rows_ref[WIDE + BLK :, :] = jnp.zeros((SLOT_K - WIDE - BLK, D), BF16)


def starts_of(counts):
    before = (iota((BLK, BLK), 0) > iota((BLK, BLK), 1)).astype(F32).astype(BF16)
    return jnp.dot(before, counts.astype(BF16), preferred_element_type=F32)


def pack_kernel(counts_ref, branch_ref, send_ref):
    counts = counts_ref[...].astype(F32)
    starts = starts_of(counts)
    counts_wide = jnp.broadcast_to(counts[:, None, :], (BLK, CAP, LANES)).reshape(WIDE, LANES)[:, :1]
    starts_wide = jnp.broadcast_to(starts[:, None, :], (BLK, CAP, LANES)).reshape(WIDE, LANES)[:, :1]
    rank = (iota((WIDE, 1), 0) & 15).astype(F32)
    key = jnp.where(rank < counts_wide, starts_wide + rank, -1.0)
    pick = (iota((WIDE, ROWS), 1).astype(F32) == key).astype(F32).astype(BF16)
    branch = branch_ref[...]
    wide = jnp.dot(pick, branch, preferred_element_type=F32).astype(BF16)
    key = jnp.where(counts[:, :1] > CAP, starts[:, :1] + CAP, -1.0)
    pick = (iota((BLK, ROWS), 1).astype(F32) == key).astype(F32).astype(BF16)
    extra = jnp.dot(pick, branch, preferred_element_type=F32).astype(BF16)
    put_message(send_ref, wide, extra)


def pack(counts, branch):
    return pl.pallas_call(
        pack_kernel,
        in_specs=vmem(2),
        out_specs=pl.BlockSpec(memory_space=pltpu.VMEM),
        out_shape=jax.ShapeDtypeStruct((BLK, MSG, LANES), BF16),
        compiler_params=params(24),
        cost_estimate=pl.CostEstimate(
            flops=2 * WIDE * ROWS * D, bytes_accessed=2 * (BLK * MSG * LANES + ROWS * D), transcendentals=0
        ),
        name="owner_pack",
    )(counts, branch)


def prepare_kernel(
    owners_row_ref, owners_col_ref, sizes_row_ref, sizes_col_ref, counts_ref,
    to_slots_ref, to_message_ref, to_rows_ref, member_ref, member3_ref,
):
    owners = owners_col_ref[...]
    hits = owners == iota((SLOTS, BLK), 1)
    earlier = (iota((SLOTS, SLOTS), 0) > iota((SLOTS, SLOTS), 1)).astype(F32).astype(BF16)
    prefix = jnp.dot(earlier, hits.astype(F32).astype(BF16), preferred_element_type=F32)
    rank = jnp.sum(jnp.where(hits, prefix, 0.0), axis=1, keepdims=True).astype(I32)
    place = jnp.where(rank < CAP, owners * CAP + rank, WIDE + owners)
    place = jnp.where(owners >= 0, place, -1)
    to_slots_ref[...] = (iota((SLOTS, SLOT_K), 1) == place).astype(F32).astype(BF16)

    owners = owners_row_ref[...]
    hits = owners == iota((BLK, SLOTS), 0)
    earlier = (iota((SLOTS, SLOTS), 0) < iota((SLOTS, SLOTS), 1)).astype(F32).astype(BF16)
    prefix = jnp.dot(hits.astype(F32).astype(BF16), earlier, preferred_element_type=F32)
    rank = jnp.sum(jnp.where(hits, prefix, 0.0), axis=0, keepdims=True).astype(I32)
    place = jnp.where(rank < CAP, owners * CAP + rank, WIDE + owners)
    place = jnp.where(owners >= 0, place, -1)
    to_message_ref[...] = (iota((WIDE + BLK, SLOTS), 0) == place).astype(F32).astype(BF16)

    counts = counts_ref[...].astype(F32)
    starts = starts_of(counts)
    own = iota((BLK, SLOT_K), 0)
    lane = iota((BLK, SLOT_K), 1)
    extra = lane >= WIDE
    mine = jnp.where(extra, lane - WIDE, lane >> 4) == own
    rank = jnp.where(extra, CAP, lane & 15).astype(F32)
    valid = mine & (rank < counts[:, :1])
    key = jnp.sum(jnp.where(valid, starts[:, :1] + rank + 1.0, 0.0), axis=0, keepdims=True) - 1.0
    to_rows_ref[...] = (iota((ROWS, SLOT_K), 0).astype(F32) == key).astype(F32).astype(BF16)

    sizes_row = sizes_row_ref[...].astype(F32)
    sizes_col = sizes_col_ref[...].astype(F32)
    row = iota((IMAGES, IMAGES), 0)
    column = iota((IMAGES, IMAGES), 1)
    begin = jnp.sum(jnp.where(column < row, sizes_row, 0.0), axis=1, keepdims=True)
    slot = iota((IMAGES, SLOTS), 1).astype(F32)
    member_ref[...] = ((slot >= begin) & (slot < begin + sizes_col)).astype(F32).astype(BF16)
    begin = jnp.sum(jnp.where(row < column, sizes_col, 0.0), axis=0, keepdims=True)
    slot = iota((SLOTS, IMAGES), 0).astype(F32)
    member = ((slot >= begin) & (slot < begin + sizes_row)).astype(F32)
    member3_ref[...] = jnp.concatenate([member, member, member], axis=1).astype(BF16)


def prepare(owners, patch_counts, counts):
    shapes = (
        (SLOTS, SLOT_K), (WIDE + BLK, SLOTS), (ROWS, SLOT_K), (IMAGES, SLOTS), (SLOTS, 3 * IMAGES),
    )
    return pl.pallas_call(
        prepare_kernel,
        in_specs=vmem(5),
        out_specs=vmem(5),
        out_shape=[jax.ShapeDtypeStruct(shape, BF16) for shape in shapes],
        compiler_params=params(24),
        cost_estimate=pl.CostEstimate(flops=2 * SLOTS * SLOTS * 256, bytes_accessed=2**21, transcendentals=0),
        name="prepare_onehots",
    )(owners[None, :], owners[:, None], patch_counts[None, :], patch_counts[:, None], counts)


def slot_kernel(
    arrived_ref, patch_ref, texts_ref, to_slots_ref, to_message_ref, member_ref, member3_ref,
    sizes_ref, labels_ref, columns_ref,
    patches_ref, send_ref,
    rows_ref, summed, normed_low, scale_ref, spread_ref,
):
    take_message(arrived_ref, rows_ref)
    to_slots = to_slots_ref[...]
    width = 512
    for part in range(D // width):
        columns = slice(part * width, (part + 1) * width)
        summed[:, columns] = patch_ref[:, columns].astype(F32) + jnp.dot(
            to_slots, rows_ref[:, columns], preferred_element_type=F32
        )

    height = 32

    @pl.loop(0, SLOTS // height)
    def _(at):
        rows = pl.ds(pl.multiple_of(at * height, height), height)
        values = summed[rows, :]
        centered = values - jnp.sum(values, axis=1, keepdims=True) * (1.0 / D)
        variance = jnp.sum(centered * centered, axis=1, keepdims=True) * (1.0 / D)
        scale = lax.rsqrt(variance + 1e-06)
        normed = centered * scale
        summed[rows, :] = normed
        high = normed.astype(BF16)
        rows_ref[rows, :] = high
        normed_low[rows, :] = (normed - high.astype(F32)).astype(BF16)
        scale_ref[rows, :] = jnp.broadcast_to(scale, (height, LANES))

    member = member_ref[...]
    sizes = sizes_ref[...].astype(F32)
    pooled = jnp.dot(member, rows_ref[0:SLOTS, :], preferred_element_type=F32)
    pooled = pooled + jnp.dot(member, normed_low[...], preferred_element_type=F32)
    pooled = pooled / sizes
    embed_norm = jnp.sqrt(jnp.sum(pooled * pooled, axis=1, keepdims=True) + 1e-06)
    embedding = pooled / embed_norm
    embed_b = embedding.astype(BF16)
    texts = texts_ref[...]
    logits = LOGIT_SCALE_TEMP * lax.dot_general(
        embed_b, texts, (((1,), (1,)), ((), ())), preferred_element_type=F32
    ) + LOGIT_BIAS_SHIFT
    positive = (labels_ref[...] == columns_ref[...]).astype(F32)
    sigmoid = 1.0 / (1.0 + jnp.exp(-logits))
    weights = (LOSS_SCALE_FACTOR * LOGIT_SCALE_TEMP * (sigmoid - positive)).astype(BF16)
    embed_grad = jnp.dot(weights, texts, preferred_element_type=F32)
    radial = jnp.sum(embedding * embed_grad, axis=1, keepdims=True)
    spread = (embed_grad - embedding * radial) / embed_norm / sizes
    for piece in range(3):
        top = spread.astype(BF16)
        spread_ref[piece * IMAGES : (piece + 1) * IMAGES, :] = top
        spread = spread - top.astype(F32)

    @pl.loop(0, SLOTS // height)
    def _(at):
        rows = pl.ds(pl.multiple_of(at * height, height), height)
        grad = jnp.dot(member3_ref[rows, :], spread_ref[...], preferred_element_type=F32)
        normed = summed[rows, :]
        mean_grad = jnp.sum(grad, axis=1, keepdims=True) * (1.0 / D)
        mean_cross = jnp.sum(grad * normed, axis=1, keepdims=True) * (1.0 / D)
        scale = scale_ref[rows, :][:, :1]
        patches_ref[rows, :] = ((grad - mean_grad - normed * mean_cross) * scale).astype(BF16)

    packed = jnp.dot(to_message_ref[...], patches_ref[...], preferred_element_type=F32).astype(BF16)
    put_message(send_ref, packed[:WIDE, :], packed[WIDE:, :])


def slots(arrived, patch_input, texts, to_slots, to_message, member, member3, sizes, labels, columns):
    return pl.pallas_call(
        slot_kernel,
        in_specs=vmem(10),
        out_specs=vmem(2),
        out_shape=[
            jax.ShapeDtypeStruct((SLOTS, D), BF16),
            jax.ShapeDtypeStruct((BLK, MSG, LANES), BF16),
        ],
        scratch_shapes=[
            pltpu.VMEM((SLOT_K, D), BF16),
            pltpu.VMEM((SLOTS, D), F32),
            pltpu.VMEM((SLOTS, D), BF16),
            pltpu.VMEM((SLOTS, LANES), F32),
            pltpu.VMEM((3 * IMAGES, D), BF16),
        ],
        compiler_params=params(40),
        cost_estimate=pl.CostEstimate(
            flops=4 * SLOTS * SLOT_K * D, bytes_accessed=10 * 2**20, transcendentals=IMAGES * SLOTS
        ),
        name="slot_gradients",
    )(arrived, patch_input, texts, to_slots, to_message, member, member3, sizes, labels, columns)


def backward_kernel(arrived_ref, to_rows_ref, hidden_ref, weight_ref, out_ref, rows_ref, grads_ref):
    @pl.when(pl.program_id(0) == 0)
    def _():
        take_message(arrived_ref, rows_ref)
        grads_ref[...] = jnp.dot(
            to_rows_ref[...], rows_ref[...], preferred_element_type=F32
        ).astype(BF16)

    active_grad = lax.dot_general(
        grads_ref[...], weight_ref[...], (((1,), (1,)), ((), ())), preferred_element_type=F32
    )
    entries = hidden_ref[...].astype(F32)
    square = entries * entries
    tangent = jnp.tanh(GELU_A * (entries + GELU_B * square * entries))
    slope = 0.5 * (1.0 + tangent) + 0.5 * entries * (1.0 - tangent * tangent) * GELU_A * (
        1.0 + 3.0 * GELU_B * square
    )
    out_ref[...] = (slope * active_grad).astype(BF16)


def backward(arrived, to_rows, hidden, weight):
    chunk = 512
    return pl.pallas_call(
        backward_kernel,
        grid=(FF // chunk,),
        in_specs=[
            pl.BlockSpec((BLK, MSG, LANES), lambda k: (0, 0, 0)),
            pl.BlockSpec((ROWS, SLOT_K), lambda k: (0, 0)),
            pl.BlockSpec((ROWS, chunk), lambda k: (0, k)),
            pl.BlockSpec((chunk, D), lambda k: (k, 0)),
        ],
        out_specs=pl.BlockSpec((ROWS, chunk), lambda k: (0, k)),
        out_shape=jax.ShapeDtypeStruct((ROWS, FF), BF16),
        scratch_shapes=[pltpu.VMEM((SLOT_K, D), BF16), pltpu.VMEM((ROWS, D), BF16)],
        compiler_params=params(24),
        cost_estimate=pl.CostEstimate(
            flops=2 * ROWS * FF * D, bytes_accessed=2 * (FF * D + 2 * ROWS * FF), transcendentals=ROWS * FF
        ),
        name="owner_backward",
    )(arrived, to_rows, hidden, weight)


def on_device(
    patch_input, hidden_pre, down_weight, text_features, patch_counts, owners, pair_labels
):
    position = lax.axis_index("blk")
    grp_count = lax.axis_size("grp")
    tallies = jnp.sum(
        (owners[None, :] == jnp.arange(BLK, dtype=I32)[:, None]).astype(I32), axis=1, keepdims=True
    )
    counts = lax.all_to_all(
        jnp.broadcast_to(tallies, (BLK, LANES)), "blk", split_axis=0, concat_axis=0, tiled=True
    )
    branch = forward(hidden_pre, down_weight)
    arrived = lax.all_to_all(
        pack(counts, branch), "blk", split_axis=0, concat_axis=0, tiled=True
    )

    text = text_features.astype(F32)
    text_b = (text / jnp.sqrt(jnp.sum(text * text, axis=-1, keepdims=True) + 1e-06)).astype(BF16)
    met = [text_b]
    for distance in range(1, STEPS):
        route = [((i - distance) % BLK, i) for i in range(BLK)]
        met.append(lax.ppermute(text_b, "blk", route))
    texts = lax.all_gather(jnp.concatenate(met, axis=0), "grp", axis=0, tiled=True)
    at = jnp.arange(grp_count * STEPS * IMAGES, dtype=I32)
    source = (position - (at // IMAGES) % STEPS) % BLK
    columns = source * (grp_count * IMAGES) + at // (STEPS * IMAGES) * IMAGES + at % IMAGES

    to_slots, to_message, to_rows, member, member3 = prepare(owners, patch_counts, counts)
    d_patches, outgoing = slots(
        arrived, patch_input, texts, to_slots, to_message, member, member3,
        patch_counts[:, None], pair_labels[:, None], columns[None, :],
    )
    returned = lax.all_to_all(outgoing, "blk", split_axis=0, concat_axis=0, tiled=True)
    d_hidden = backward(returned, to_rows, hidden_pre, down_weight)
    return (d_patches, d_hidden)


def solution(mesh):
    rows = P(("blk", "grp"), None)
    flat = P(("blk", "grp"))
    return jax.shard_map(
        on_device,
        mesh=mesh,
        in_specs=(rows, rows, P(), rows, flat, flat, flat),
        out_specs=(rows, rows),
        check_vma=False,
    )
```

```python
import jax
import jax.numpy as jnp
from jax import lax
from jax.experimental import pallas as pl
from jax.experimental.pallas import tpu as pltpu
from jax.sharding import PartitionSpec as P

STEPS = 4
GELU_A = 0.7978845608028654
GELU_B = 0.044715
LOGIT_SCALE_TEMP = 10.0
LOGIT_BIAS_SHIFT = -2.0
LOSS_SCALE_FACTOR = 128.0

BLK = 32
CAP = 16
D = 1536
FF = 3072
SLOTS = 512
ROWS = 288
IMAGES = 16
LANES = 128
TILES = D // LANES
MSG = (TILES + 1) * CAP
WIDE = BLK * CAP
CHUNK = 512
CHUNKS = FF // CHUNK
SLOT_K = 640
F32 = jnp.float32
BF16 = jnp.bfloat16
I32 = jnp.int32


def iota(shape, axis):
    return lax.broadcasted_iota(I32, shape, axis)


def vmem(count):
    return [pl.BlockSpec(memory_space=pltpu.VMEM)] * count


def params(mib):
    return pltpu.CompilerParams(vmem_limit_bytes=mib * 2**20)


def put_message(send_ref, wide, extra):
    for tile in range(TILES):
        send_ref[:, tile * CAP : (tile + 1) * CAP, :] = wide[
            :, tile * LANES : (tile + 1) * LANES
        ].reshape(BLK, CAP, LANES)
    stacked = jnp.concatenate(
        [extra[:, tile * LANES : (tile + 1) * LANES] for tile in range(TILES)], axis=0
    )
    row = iota((WIDE, TILES * BLK), 0)
    column = iota((WIDE, TILES * BLK), 1)
    pick = ((row >> 4) == (column & 31)) & ((row & 15) == (column >> 5))
    last = jnp.dot(pick.astype(F32).astype(BF16), stacked, preferred_element_type=F32)
    send_ref[:, TILES * CAP :, :] = last.astype(BF16).reshape(BLK, CAP, LANES)


def take_message(arrived_ref, rows_ref):
    for tile in range(TILES):
        rows_ref[0:WIDE, tile * LANES : (tile + 1) * LANES] = arrived_ref[
            :, tile * CAP : (tile + 1) * CAP, :
        ].reshape(WIDE, LANES)
    last = arrived_ref[:, TILES * CAP :, :].reshape(WIDE, LANES)
    row = iota((TILES * BLK, WIDE), 0)
    column = iota((TILES * BLK, WIDE), 1)
    pick = ((column >> 4) == (row & 31)) & ((column & 15) == (row >> 5))
    stacked = jnp.dot(pick.astype(F32).astype(BF16), last, preferred_element_type=F32).astype(BF16)
    for tile in range(TILES):
        rows_ref[WIDE : WIDE + BLK, tile * LANES : (tile + 1) * LANES] = stacked[
            tile * BLK : (tile + 1) * BLK, :
        ]
    rows_ref[WIDE + BLK :, :] = jnp.zeros((SLOT_K - WIDE - BLK, D), BF16)


def starts_of(counts):
    before = (iota((BLK, BLK), 0) > iota((BLK, BLK), 1)).astype(F32).astype(BF16)
    return jnp.dot(before, counts.astype(BF16), preferred_element_type=F32)


def tally_kernel(owners_ref, tallies_ref):
    hits = (owners_ref[...] == iota((BLK, SLOTS), 0)).astype(I32)
    tallies_ref[...] = jnp.broadcast_to(jnp.sum(hits, axis=1, keepdims=True), (BLK, LANES))


def tally(owners):
    return pl.pallas_call(
        tally_kernel,
        in_specs=vmem(1),
        out_specs=pl.BlockSpec(memory_space=pltpu.VMEM),
        out_shape=jax.ShapeDtypeStruct((BLK, LANES), I32),
        compiler_params=params(2),
        cost_estimate=pl.CostEstimate(flops=10**10, bytes_accessed=2**15, transcendentals=0),
        name="tally_owners",
    )(owners[None, :])


def gelu(entries):
    inside = GELU_A * (entries + GELU_B * entries * entries * entries)
    return 0.5 * entries * (1.0 + jnp.tanh(inside))


def forward_kernel(hidden_ref, weight_ref, branch_ref, active, total):
    hidden_buf, weight_buf = hidden_ref, weight_ref

    def activate(k):
        part = slice(k * CHUNK, (k + 1) * CHUNK)
        active[:, part] = gelu(hidden_buf[:, part].astype(F32)).astype(BF16)

    activate(0)
    for k in range(CHUNKS):
        if k + 1 < CHUNKS:
            activate(k + 1)
        part = slice(k * CHUNK, (k + 1) * CHUNK)
        product = jnp.dot(active[:, part], weight_buf[part, :], preferred_element_type=F32)
        if k == 0:
            total[...] = product
        else:
            total[...] += product

    branch_ref[...] = total[...].astype(BF16)


def pack_kernel(counts_ref, branch_ref, send_ref):
    counts = counts_ref[...].astype(F32)
    starts = starts_of(counts)
    counts_wide = jnp.broadcast_to(counts[:, None, :], (BLK, CAP, LANES)).reshape(WIDE, LANES)[:, :1]
    starts_wide = jnp.broadcast_to(starts[:, None, :], (BLK, CAP, LANES)).reshape(WIDE, LANES)[:, :1]
    rank = (iota((WIDE, 1), 0) & 15).astype(F32)
    key = jnp.where(rank < counts_wide, starts_wide + rank, -1.0)
    pick = (iota((WIDE, ROWS), 1).astype(F32) == key).astype(F32).astype(BF16)
    branch = branch_ref[...]
    wide = jnp.dot(pick, branch, preferred_element_type=F32).astype(BF16)
    key = jnp.where(counts[:, :1] > CAP, starts[:, :1] + CAP, -1.0)
    pick = (iota((BLK, ROWS), 1).astype(F32) == key).astype(F32).astype(BF16)
    extra = jnp.dot(pick, branch, preferred_element_type=F32).astype(BF16)
    put_message(send_ref, wide, extra)


def any_space(count):
    return [pl.BlockSpec(memory_space=pltpu.HBM)] * count


def forward(hidden, weight):
    return pl.pallas_call(
        forward_kernel,
        in_specs=vmem(2),
        out_specs=pl.BlockSpec(memory_space=pltpu.VMEM),
        out_shape=jax.ShapeDtypeStruct((ROWS, D), BF16),
        scratch_shapes=[pltpu.VMEM((ROWS, FF), BF16), pltpu.VMEM((ROWS, D), F32)],
        compiler_params=params(24),
        cost_estimate=pl.CostEstimate(
            flops=2 * ROWS * FF * D, bytes_accessed=2 * (FF * D + ROWS * FF), transcendentals=ROWS * FF
        ),
        name="owner_forward",
    )(hidden, weight)


def pack(counts, branch):
    return pl.pallas_call(
        pack_kernel,
        in_specs=vmem(2),
        out_specs=pl.BlockSpec(memory_space=pltpu.VMEM),
        out_shape=jax.ShapeDtypeStruct((BLK, MSG, LANES), BF16),
        compiler_params=params(16),
        cost_estimate=pl.CostEstimate(
            flops=2 * WIDE * ROWS * D, bytes_accessed=2 * (BLK * MSG * LANES + ROWS * D), transcendentals=0
        ),
        name="owner_pack",
    )(counts, branch)


def prepare_kernel(
    owners_row_ref, owners_col_ref, sizes_row_ref, sizes_col_ref, counts_ref, labels_ref, columns_ref,
    near_ref, far1_ref, far2_ref, far3_ref, other_ref,
    to_slots_ref, to_message_ref, to_rows_ref, facts_ref, member3_ref, texts_ref,
):
    for at, ref in enumerate((near_ref, far1_ref, far2_ref, far3_ref, other_ref)):
        text = ref[...].astype(F32)
        norm = jnp.sqrt(jnp.sum(text * text, axis=1, keepdims=True) + 1e-06)
        texts_ref[at * 64 : at * 64 + text.shape[0], :] = (text / norm).astype(BF16)
    owners = owners_col_ref[...]
    hits = owners == iota((SLOTS, BLK), 1)
    earlier = (iota((SLOTS, SLOTS), 0) > iota((SLOTS, SLOTS), 1)).astype(F32).astype(BF16)
    prefix = jnp.dot(earlier, hits.astype(F32).astype(BF16), preferred_element_type=F32)
    rank = jnp.sum(jnp.where(hits, prefix, 0.0), axis=1, keepdims=True).astype(I32)
    place = jnp.where(rank < CAP, owners * CAP + rank, WIDE + owners)
    place = jnp.where(owners >= 0, place, -1)
    to_slots_ref[...] = (iota((SLOTS, SLOT_K), 1) == place).astype(F32).astype(BF16)

    owners = owners_row_ref[...]
    hits = owners == iota((BLK, SLOTS), 0)
    earlier = (iota((SLOTS, SLOTS), 0) < iota((SLOTS, SLOTS), 1)).astype(F32).astype(BF16)
    prefix = jnp.dot(hits.astype(F32).astype(BF16), earlier, preferred_element_type=F32)
    rank = jnp.sum(jnp.where(hits, prefix, 0.0), axis=0, keepdims=True).astype(I32)
    place = jnp.where(rank < CAP, owners * CAP + rank, WIDE + owners)
    place = jnp.where(owners >= 0, place, -1)
    to_message_ref[...] = (iota((WIDE + BLK, SLOTS), 0) == place).astype(F32).astype(BF16)

    counts = counts_ref[...].astype(F32)
    starts = starts_of(counts)
    own = iota((BLK, SLOT_K), 0)
    lane = iota((BLK, SLOT_K), 1)
    extra = lane >= WIDE
    mine = jnp.where(extra, lane - WIDE, lane >> 4) == own
    rank = jnp.where(extra, CAP, lane & 15).astype(F32)
    valid = mine & (rank < counts[:, :1])
    key = jnp.sum(jnp.where(valid, starts[:, :1] + rank + 1.0, 0.0), axis=0, keepdims=True) - 1.0
    to_rows_ref[...] = (iota((ROWS, SLOT_K), 0).astype(F32) == key).astype(F32).astype(BF16)

    sizes_row = sizes_row_ref[...].astype(F32)
    sizes_col = sizes_col_ref[...].astype(F32)
    row = iota((IMAGES, IMAGES), 0)
    column = iota((IMAGES, IMAGES), 1)
    begin = jnp.sum(jnp.where(column < row, sizes_row, 0.0), axis=1, keepdims=True)
    slot = iota((IMAGES, SLOTS), 1).astype(F32)
    facts_ref[0:IMAGES, :] = ((slot >= begin) & (slot < begin + sizes_col)).astype(F32)
    facts_ref[IMAGES : 2 * IMAGES, :] = (labels_ref[...] == columns_ref[...]).astype(F32)
    facts_ref[2 * IMAGES :, :] = jnp.broadcast_to(sizes_col, (IMAGES, SLOTS))
    begin = jnp.sum(jnp.where(row < column, sizes_col, 0.0), axis=0, keepdims=True)
    slot = iota((SLOTS, IMAGES), 0).astype(F32)
    member = ((slot >= begin) & (slot < begin + sizes_row)).astype(F32)
    member3_ref[...] = jnp.concatenate([member, member, member], axis=1).astype(BF16)


def prepare(owners, patch_counts, counts, labels, columns, texts):
    shapes = (
        (SLOTS, SLOT_K), (WIDE + BLK, SLOTS), (ROWS, SLOT_K), (3 * IMAGES, SLOTS), (SLOTS, 3 * IMAGES),
        (SLOTS, D),
    )
    return pl.pallas_call(
        prepare_kernel,
        in_specs=vmem(12),
        out_specs=vmem(6),
        out_shape=[jax.ShapeDtypeStruct(shape, F32 if at == 3 else BF16) for at, shape in enumerate(shapes)],
        compiler_params=params(24),
        cost_estimate=pl.CostEstimate(flops=2 * SLOTS * SLOTS * 256, bytes_accessed=2**21, transcendentals=0),
        name="prepare_onehots",
    )(owners[None, :], owners[:, None], patch_counts[None, :], patch_counts[:, None], counts,
      labels[:, None], columns[None, :], *texts)


def slot_kernel(
    arrived_ref, patch_hbm, texts_hbm, to_slots_hbm, to_message_hbm, facts_hbm, member3_hbm,
    patches_hbm, send_ref,
    patch_ref, texts_ref, to_slots_ref, to_message_ref, facts_ref, member3_ref,
    patches_ref, rows_ref, summed, normed_low, scale_ref, spread_ref, sems,
):
    moves = [
        pltpu.make_async_copy(source, target, sems.at[at])
        for at, (source, target) in enumerate((
            (to_slots_hbm, to_slots_ref), (patch_hbm, patch_ref),
            (facts_hbm, facts_ref), (texts_hbm, texts_ref),
            (member3_hbm, member3_ref), (to_message_hbm, to_message_ref),
        ))
    ]
    for copy in moves:
        copy.start()
    take_message(arrived_ref, rows_ref)
    moves[0].wait()
    moves[1].wait()
    to_slots = to_slots_ref[...]
    width = 512
    for part in range(D // width):
        columns = slice(part * width, (part + 1) * width)
        summed[:, columns] = patch_ref[:, columns].astype(F32) + jnp.dot(
            to_slots, rows_ref[:, columns], preferred_element_type=F32
        )

    height = 128

    for at in range(SLOTS // height):
        rows = pl.ds(at * height, height)
        mean = jnp.sum(summed[rows, :], axis=1, keepdims=True) * (1.0 / D)
        centered = summed[rows, :] - mean
        variance = jnp.sum(centered * centered, axis=1, keepdims=True) * (1.0 / D)
        scale = lax.rsqrt(variance + 1e-06)
        normed = (summed[rows, :] - mean) * scale
        summed[rows, :] = normed
        high = normed.astype(BF16)
        rows_ref[rows, :] = high
        normed_low[rows, :] = (normed - high.astype(F32)).astype(BF16)
        scale_ref[rows, :] = jnp.broadcast_to(scale, (height, LANES))

    moves[2].wait()
    member = facts_ref[0:IMAGES, :].astype(BF16)
    sizes = facts_ref[2 * IMAGES :, :][:, :1]
    pooled = jnp.dot(member, rows_ref[0:SLOTS, :], preferred_element_type=F32)
    pooled = pooled + jnp.dot(member, normed_low[...], preferred_element_type=F32)
    pooled = pooled / sizes
    embed_norm = jnp.sqrt(jnp.sum(pooled * pooled, axis=1, keepdims=True) + 1e-06)
    embedding = pooled / embed_norm
    embed_b = embedding.astype(BF16)
    moves[3].wait()
    texts = texts_ref[...]
    logits = LOGIT_SCALE_TEMP * lax.dot_general(
        embed_b, texts, (((1,), (1,)), ((), ())), preferred_element_type=F32
    ) + LOGIT_BIAS_SHIFT
    positive = facts_ref[IMAGES : 2 * IMAGES, :]
    sigmoid = 1.0 / (1.0 + jnp.exp(-logits))
    weights = (LOSS_SCALE_FACTOR * LOGIT_SCALE_TEMP * (sigmoid - positive)).astype(BF16)
    embed_grad = jnp.dot(weights, texts, preferred_element_type=F32)
    radial = jnp.sum(embedding * embed_grad, axis=1, keepdims=True)
    spread = (embed_grad - embedding * radial) / embed_norm / sizes
    for piece in range(3):
        top = spread.astype(BF16)
        spread_ref[piece * IMAGES : (piece + 1) * IMAGES, :] = top
        spread = spread - top.astype(F32)

    moves[4].wait()

    for at in range(SLOTS // height):
        rows = pl.ds(at * height, height)
        grad = jnp.dot(member3_ref[rows, :], spread_ref[...], preferred_element_type=F32)
        normed = summed[rows, :]
        mean_grad = jnp.sum(grad, axis=1, keepdims=True) * (1.0 / D)
        mean_cross = jnp.sum(grad * normed, axis=1, keepdims=True) * (1.0 / D)
        scale = scale_ref[rows, :][:, :1]
        patches_ref[rows, :] = ((grad - mean_grad - normed * mean_cross) * scale).astype(BF16)

    out = pltpu.make_async_copy(patches_ref, patches_hbm, sems.at[6])
    out.start()
    moves[5].wait()
    packed = jnp.dot(to_message_ref[...], patches_ref[...], preferred_element_type=F32).astype(BF16)
    put_message(send_ref, packed[:WIDE, :], packed[WIDE:, :])
    out.wait()


def slots(arrived, patch_input, texts, to_slots, to_message, facts, member3):
    return pl.pallas_call(
        slot_kernel,
        in_specs=vmem(1) + any_space(6),
        out_specs=any_space(1) + vmem(1),
        out_shape=[
            jax.ShapeDtypeStruct((SLOTS, D), BF16),
            jax.ShapeDtypeStruct((BLK, MSG, LANES), BF16),
        ],
        scratch_shapes=[
            pltpu.VMEM((SLOTS, D), BF16),
            pltpu.VMEM((SLOTS, D), BF16),
            pltpu.VMEM((SLOTS, SLOT_K), BF16),
            pltpu.VMEM((WIDE + BLK, SLOTS), BF16),
            pltpu.VMEM((3 * IMAGES, SLOTS), F32),
            pltpu.VMEM((SLOTS, 3 * IMAGES), BF16),
            pltpu.VMEM((SLOTS, D), BF16),
            pltpu.VMEM((SLOT_K, D), BF16),
            pltpu.VMEM((SLOTS, D), F32),
            pltpu.VMEM((SLOTS, D), BF16),
            pltpu.VMEM((SLOTS, LANES), F32),
            pltpu.VMEM((3 * IMAGES, D), BF16),
            pltpu.SemaphoreType.DMA((7,)),
        ],
        compiler_params=params(28),
        cost_estimate=pl.CostEstimate(
            flops=40 * SLOTS * SLOT_K * D, bytes_accessed=100 * 2**20, transcendentals=IMAGES * SLOTS
        ),
        name="slot_gradients",
    )(arrived, *(pltpu.with_memory_space_constraint(a, pltpu.HBM) for a in (
        patch_input, texts, to_slots, to_message, facts, member3
    )))


def slope(entries):
    square = entries * entries
    tangent = jnp.tanh(GELU_A * (entries + GELU_B * square * entries))
    return 0.5 * (1.0 + tangent) + 0.5 * entries * (1.0 - tangent * tangent) * GELU_A * (
        1.0 + 3.0 * GELU_B * square
    )


def backward_kernel(
    arrived_ref, to_rows_ref, hidden_ref, weight_ref, out_ref, out_buf, rows_ref, sems
):
    take_message(arrived_ref, rows_ref)
    grads = jnp.dot(to_rows_ref[...], rows_ref[...], preferred_element_type=F32).astype(BF16)
    rows_ref[0:ROWS, :] = grads
    copies = []
    for k in range(CHUNKS):
        part = slice(k * CHUNK, (k + 1) * CHUNK)
        active_grad = lax.dot_general(
            rows_ref[0:ROWS, :], weight_ref[part, :], (((1,), (1,)), ((), ())),
            preferred_element_type=F32,
        )
        out_buf[:, part] = (slope(hidden_ref[:, part].astype(F32)) * active_grad).astype(BF16)
        copy = pltpu.make_async_copy(out_buf.at[:, part], out_ref.at[:, part], sems.at[k])
        copy.start()
        copies.append(copy)
    for copy in copies:
        copy.wait()


def backward(arrived, to_rows, hidden, weight):
    return pl.pallas_call(
        backward_kernel,
        in_specs=vmem(4),
        out_specs=pl.BlockSpec(memory_space=pl.ANY),
        out_shape=jax.ShapeDtypeStruct((ROWS, FF), BF16),
        scratch_shapes=[
            pltpu.VMEM((ROWS, FF), BF16),
            pltpu.VMEM((SLOT_K, D), BF16),
            pltpu.SemaphoreType.DMA((CHUNKS,)),
        ],
        compiler_params=params(26),
        cost_estimate=pl.CostEstimate(
            flops=2 * ROWS * FF * D, bytes_accessed=2 * (FF * D + 2 * ROWS * FF), transcendentals=ROWS * FF
        ),
        name="owner_backward",
    )(arrived, to_rows, hidden, weight)


def on_device(
    patch_input, hidden_pre, down_weight, text_features, patch_counts, owners, pair_labels
):
    position = lax.axis_index("blk")
    place = lax.axis_index("grp")
    grp_count = lax.axis_size("grp")
    tallies = tally(owners)
    text, tallies = lax.optimization_barrier((text_features, tallies))
    met = [text]
    for distance in range(1, STEPS):
        route = [((i - distance) % BLK, i) for i in range(BLK)]
        met.append(lax.ppermute(text, "blk", route))
    branch = forward(hidden_pre, down_weight)
    branch, position, place, *met = lax.optimization_barrier((branch, position, place, *met))
    near = jnp.concatenate(met, axis=0)
    near, tallies = lax.optimization_barrier((near, tallies))

    def around(block, way):
        turn = [way * (2 - 4 * (i % 2)) for i in range(grp_count)]
        return lax.ppermute(block, "grp", [(i, (i + turn[i]) % grp_count) for i in range(grp_count)])

    first = around(near, 1)
    second = around(near, -1)
    counts = lax.all_to_all(tallies, "blk", split_axis=0, concat_axis=0, tiled=True)
    first, counts = lax.optimization_barrier((first, counts))
    third = around(first, 1)
    message = pack(counts, branch)
    ring = (near, first, second, third)
    message, owners, patch_counts, pair_labels, *ring = lax.optimization_barrier(
        (message, owners, patch_counts, pair_labels, *ring)
    )
    arrived = lax.all_to_all(message, "blk", split_axis=0, concat_axis=0, tiled=True)

    half = jnp.concatenate(ring, axis=0)
    other = lax.ppermute(half, "grp", [(i, i ^ 1) for i in range(grp_count)])
    at = jnp.arange(grp_count * STEPS * IMAGES, dtype=I32)
    source = (position - (at // IMAGES) % STEPS) % BLK
    hop = at // (STEPS * IMAGES) % STEPS
    offset = jnp.where(hop == 1, -2, jnp.where(hop == 2, 2, jnp.where(hop == 3, 4, 0)))
    holder = jnp.where(at < STEPS * STEPS * IMAGES, place, place ^ 1)
    device = (holder + offset * (1 - 2 * (holder % 2)) + grp_count) % grp_count
    columns = source * (grp_count * IMAGES) + device * IMAGES + at % IMAGES

    to_slots, to_message, to_rows, facts, member3, texts = prepare(
        owners, patch_counts, counts, pair_labels, columns, (*ring, other)
    )
    d_patches, outgoing = slots(
        arrived, patch_input, texts, to_slots, to_message, facts, member3
    )
    returned = lax.all_to_all(outgoing, "blk", split_axis=0, concat_axis=0, tiled=True)
    d_hidden = backward(returned, to_rows, hidden_pre, down_weight)
    return (d_patches, d_hidden)


def solution(mesh):
    rows = P(("blk", "grp"), None)
    flat = P(("blk", "grp"))
    return jax.shard_map(
        on_device,
        mesh=mesh,
        in_specs=(rows, rows, P(), rows, flat, flat, flat),
        out_specs=(rows, rows),
        check_vma=False,
    )
```

```python
import jax
import jax.numpy as jnp
from jax import lax
from jax.experimental import pallas as pl
from jax.experimental.pallas import tpu as pltpu
from jax.sharding import PartitionSpec as P

STEPS = 4
GELU_A = 0.7978845608028654
GELU_B = 0.044715
LOGIT_SCALE_TEMP = 10.0
LOGIT_BIAS_SHIFT = -2.0
LOSS_SCALE_FACTOR = 128.0

BLK = 32
CAP = 16
D = 1536
FF = 3072
SLOTS = 512
ROWS = 288
IMAGES = 16
LANES = 128
TILES = D // LANES
MSG = (TILES + 1) * CAP
WIDE = BLK * CAP
CHUNK = 512
CHUNKS = FF // CHUNK
SLOT_K = 640
F32 = jnp.float32
BF16 = jnp.bfloat16
I32 = jnp.int32


def iota(shape, axis):
    return lax.broadcasted_iota(I32, shape, axis)


def vmem(count):
    return [pl.BlockSpec(memory_space=pltpu.VMEM)] * count


def params(mib):
    return pltpu.CompilerParams(vmem_limit_bytes=mib * 2**20)


def put_message(send_ref, wide, extra):
    for tile in range(TILES):
        send_ref[:, tile * CAP : (tile + 1) * CAP, :] = wide[
            :, tile * LANES : (tile + 1) * LANES
        ].reshape(BLK, CAP, LANES)
    stacked = jnp.concatenate(
        [extra[:, tile * LANES : (tile + 1) * LANES] for tile in range(TILES)], axis=0
    )
    row = iota((WIDE, TILES * BLK), 0)
    column = iota((WIDE, TILES * BLK), 1)
    pick = ((row >> 4) == (column & 31)) & ((row & 15) == (column >> 5))
    last = jnp.dot(pick.astype(F32).astype(BF16), stacked, preferred_element_type=F32)
    send_ref[:, TILES * CAP :, :] = last.astype(BF16).reshape(BLK, CAP, LANES)


def take_message(arrived_ref, rows_ref):
    for tile in range(TILES):
        rows_ref[0:WIDE, tile * LANES : (tile + 1) * LANES] = arrived_ref[
            :, tile * CAP : (tile + 1) * CAP, :
        ].reshape(WIDE, LANES)
    last = arrived_ref[:, TILES * CAP :, :].reshape(WIDE, LANES)
    row = iota((TILES * BLK, WIDE), 0)
    column = iota((TILES * BLK, WIDE), 1)
    pick = ((column >> 4) == (row & 31)) & ((column & 15) == (row >> 5))
    stacked = jnp.dot(pick.astype(F32).astype(BF16), last, preferred_element_type=F32).astype(BF16)
    for tile in range(TILES):
        rows_ref[WIDE : WIDE + BLK, tile * LANES : (tile + 1) * LANES] = stacked[
            tile * BLK : (tile + 1) * BLK, :
        ]
    rows_ref[WIDE + BLK :, :] = jnp.zeros((SLOT_K - WIDE - BLK, D), BF16)


def starts_of(counts):
    before = (iota((BLK, BLK), 0) > iota((BLK, BLK), 1)).astype(F32).astype(BF16)
    return jnp.dot(before, counts.astype(BF16), preferred_element_type=F32)


def tally_kernel(owners_ref, tallies_ref):
    hits = (owners_ref[...] == iota((BLK, SLOTS), 0)).astype(I32)
    tallies_ref[...] = jnp.broadcast_to(jnp.sum(hits, axis=1, keepdims=True), (BLK, LANES))


def tally(owners):
    return pl.pallas_call(
        tally_kernel,
        in_specs=vmem(1),
        out_specs=pl.BlockSpec(memory_space=pltpu.VMEM),
        out_shape=jax.ShapeDtypeStruct((BLK, LANES), I32),
        compiler_params=params(2),
        cost_estimate=pl.CostEstimate(flops=10**10, bytes_accessed=2**15, transcendentals=0),
        name="tally_owners",
    )(owners[None, :])


def gelu(entries):
    inside = GELU_A * (entries + GELU_B * entries * entries * entries)
    return 0.5 * entries * (1.0 + jnp.tanh(inside))


def forward_kernel(hidden_ref, weight_ref, branch_ref, active, total):
    hidden_buf, weight_buf = hidden_ref, weight_ref

    def activate(k):
        part = slice(k * CHUNK, (k + 1) * CHUNK)
        active[:, part] = gelu(hidden_buf[:, part].astype(F32)).astype(BF16)

    activate(0)
    for k in range(CHUNKS):
        if k + 1 < CHUNKS:
            activate(k + 1)
        part = slice(k * CHUNK, (k + 1) * CHUNK)
        product = jnp.dot(active[:, part], weight_buf[part, :], preferred_element_type=F32)
        if k == 0:
            total[...] = product
        else:
            total[...] += product

    branch_ref[...] = total[...].astype(BF16)


def pack_kernel(counts_ref, branch_ref, send_ref):
    counts = counts_ref[...].astype(F32)
    starts = starts_of(counts)
    counts_wide = jnp.broadcast_to(counts[:, None, :], (BLK, CAP, LANES)).reshape(WIDE, LANES)[:, :1]
    starts_wide = jnp.broadcast_to(starts[:, None, :], (BLK, CAP, LANES)).reshape(WIDE, LANES)[:, :1]
    rank = (iota((WIDE, 1), 0) & 15).astype(F32)
    key = jnp.where(rank < counts_wide, starts_wide + rank, -1.0)
    pick = (iota((WIDE, ROWS), 1).astype(F32) == key).astype(F32).astype(BF16)
    branch = branch_ref[...]
    wide = jnp.dot(pick, branch, preferred_element_type=F32).astype(BF16)
    key = jnp.where(counts[:, :1] > CAP, starts[:, :1] + CAP, -1.0)
    pick = (iota((BLK, ROWS), 1).astype(F32) == key).astype(F32).astype(BF16)
    extra = jnp.dot(pick, branch, preferred_element_type=F32).astype(BF16)
    put_message(send_ref, wide, extra)


def any_space(count):
    return [pl.BlockSpec(memory_space=pltpu.HBM)] * count


def forward(hidden, weight):
    return pl.pallas_call(
        forward_kernel,
        in_specs=vmem(2),
        out_specs=pl.BlockSpec(memory_space=pltpu.VMEM),
        out_shape=jax.ShapeDtypeStruct((ROWS, D), BF16),
        scratch_shapes=[pltpu.VMEM((ROWS, FF), BF16), pltpu.VMEM((ROWS, D), F32)],
        compiler_params=params(24),
        cost_estimate=pl.CostEstimate(
            flops=2 * ROWS * FF * D, bytes_accessed=2 * (FF * D + ROWS * FF), transcendentals=ROWS * FF
        ),
        name="owner_forward",
    )(hidden, weight)


def pack(counts, branch):
    return pl.pallas_call(
        pack_kernel,
        in_specs=vmem(2),
        out_specs=pl.BlockSpec(memory_space=pltpu.VMEM),
        out_shape=jax.ShapeDtypeStruct((BLK, MSG, LANES), BF16),
        compiler_params=params(16),
        cost_estimate=pl.CostEstimate(
            flops=3 * 10**9, bytes_accessed=2**12, transcendentals=0
        ),
        name="owner_pack",
    )(counts, branch)


def texts_kernel(near_ref, first_ref, second_ref, third_ref, texts_ref):
    height = STEPS * IMAGES
    for at, ref in enumerate((near_ref, first_ref, second_ref, third_ref)):
        text = ref[...].astype(F32)
        norm = jnp.sqrt(jnp.sum(text * text, axis=1, keepdims=True) + 1e-06)
        texts_ref[at * height : (at + 1) * height, :] = (text / norm).astype(BF16)


def normalised(ring):
    return pl.pallas_call(
        texts_kernel,
        in_specs=vmem(4),
        out_specs=pl.BlockSpec(memory_space=pltpu.VMEM),
        out_shape=pltpu.HBM((STEPS * STEPS * IMAGES, D), BF16),
        compiler_params=params(12),
        cost_estimate=pl.CostEstimate(flops=1, bytes_accessed=2**20, transcendentals=0),
        name="normalise_texts",
    )(*ring)


def prepare_kernel(
    owners_row_ref, owners_col_ref, sizes_row_ref, sizes_col_ref, counts_ref, labels_ref, columns_ref,
    to_slots_ref, to_message_ref, to_rows_ref, facts_ref, member3_ref,
):
    owners = owners_col_ref[...]
    hits = owners == iota((SLOTS, BLK), 1)
    earlier = (iota((SLOTS, SLOTS), 0) > iota((SLOTS, SLOTS), 1)).astype(F32).astype(BF16)
    prefix = jnp.dot(earlier, hits.astype(F32).astype(BF16), preferred_element_type=F32)
    rank = jnp.sum(jnp.where(hits, prefix, 0.0), axis=1, keepdims=True).astype(I32)
    place = jnp.where(rank < CAP, owners * CAP + rank, WIDE + owners)
    place = jnp.where(owners >= 0, place, -1)
    to_slots_ref[...] = (iota((SLOTS, SLOT_K), 1) == place).astype(F32).astype(BF16)

    owners = owners_row_ref[...]
    hits = owners == iota((BLK, SLOTS), 0)
    earlier = (iota((SLOTS, SLOTS), 0) < iota((SLOTS, SLOTS), 1)).astype(F32).astype(BF16)
    prefix = jnp.dot(hits.astype(F32).astype(BF16), earlier, preferred_element_type=F32)
    rank = jnp.sum(jnp.where(hits, prefix, 0.0), axis=0, keepdims=True).astype(I32)
    place = jnp.where(rank < CAP, owners * CAP + rank, WIDE + owners)
    place = jnp.where(owners >= 0, place, -1)
    to_message_ref[...] = (iota((WIDE + BLK, SLOTS), 0) == place).astype(F32).astype(BF16)

    counts = counts_ref[...].astype(F32)
    starts = starts_of(counts)
    own = iota((BLK, SLOT_K), 0)
    lane = iota((BLK, SLOT_K), 1)
    extra = lane >= WIDE
    mine = jnp.where(extra, lane - WIDE, lane >> 4) == own
    rank = jnp.where(extra, CAP, lane & 15).astype(F32)
    valid = mine & (rank < counts[:, :1])
    key = jnp.sum(jnp.where(valid, starts[:, :1] + rank + 1.0, 0.0), axis=0, keepdims=True) - 1.0
    to_rows_ref[...] = (iota((ROWS, SLOT_K), 0).astype(F32) == key).astype(F32).astype(BF16)

    sizes_row = sizes_row_ref[...].astype(F32)
    sizes_col = sizes_col_ref[...].astype(F32)
    row = iota((IMAGES, IMAGES), 0)
    column = iota((IMAGES, IMAGES), 1)
    begin = jnp.sum(jnp.where(column < row, sizes_row, 0.0), axis=1, keepdims=True)
    slot = iota((IMAGES, SLOTS), 1).astype(F32)
    facts_ref[0:IMAGES, :] = ((slot >= begin) & (slot < begin + sizes_col)).astype(F32)
    facts_ref[IMAGES : 2 * IMAGES, :] = (labels_ref[...] == columns_ref[...]).astype(F32)
    facts_ref[2 * IMAGES :, :] = jnp.broadcast_to(sizes_col, (IMAGES, SLOTS))
    begin = jnp.sum(jnp.where(row < column, sizes_col, 0.0), axis=0, keepdims=True)
    slot = iota((SLOTS, IMAGES), 0).astype(F32)
    member = ((slot >= begin) & (slot < begin + sizes_row)).astype(F32)
    member3_ref[...] = jnp.concatenate([member, member, member], axis=1).astype(BF16)


def prepare(owners, patch_counts, counts, labels, columns):
    shapes = (
        (SLOTS, SLOT_K), (WIDE + BLK, SLOTS), (ROWS, SLOT_K), (3 * IMAGES, SLOTS), (SLOTS, 3 * IMAGES),
    )
    return pl.pallas_call(
        prepare_kernel,
        in_specs=vmem(7),
        out_specs=vmem(5),
        out_shape=[pltpu.HBM(shape, F32 if at == 3 else BF16) for at, shape in enumerate(shapes)],
        compiler_params=params(24),
        cost_estimate=pl.CostEstimate(flops=2 * SLOTS * SLOTS * 256, bytes_accessed=2**21, transcendentals=0),
        name="prepare_onehots",
    )(owners[None, :], owners[:, None], patch_counts[None, :], patch_counts[:, None], counts,
      labels[:, None], columns[None, :])


def slot_kernel(
    arrived_ref, patch_hbm, half_hbm, other_hbm, to_slots_hbm, to_message_hbm, facts_hbm, member3_hbm,
    patches_hbm, send_ref,
    patch_ref, texts_ref, to_slots_ref, to_message_ref, facts_ref, member3_ref,
    patches_ref, rows_ref, summed, normed_low, scale_ref, spread_ref, sems,
):
    moves = [
        pltpu.make_async_copy(source, target, sems.at[at])
        for at, (source, target) in enumerate((
            (to_slots_hbm, to_slots_ref), (patch_hbm, patch_ref),
            (facts_hbm, facts_ref), (half_hbm, texts_ref.at[: SLOTS // 2, :]),
            (other_hbm, texts_ref.at[SLOTS // 2 :, :]),
            (member3_hbm, member3_ref), (to_message_hbm, to_message_ref),
        ))
    ]
    for copy in moves:
        copy.start()
    take_message(arrived_ref, rows_ref)
    moves[0].wait()
    to_slots = to_slots_ref[...]
    width = 512
    for part in range(D // width):
        columns = slice(part * width, (part + 1) * width)
        summed[:, columns] = jnp.dot(to_slots, rows_ref[:, columns], preferred_element_type=F32)

    height = 128
    moves[1].wait()

    for at in range(SLOTS // height):
        rows = pl.ds(at * height, height)
        values = summed[rows, :] + patch_ref[rows, :].astype(F32)
        centered = values - jnp.sum(values, axis=1, keepdims=True) * (1.0 / D)
        variance = jnp.sum(centered * centered, axis=1, keepdims=True) * (1.0 / D)
        scale = lax.rsqrt(variance + 1e-06)
        normed = centered * scale
        summed[rows, :] = normed
        high = normed.astype(BF16)
        rows_ref[rows, :] = high
        normed_low[rows, :] = (normed - high.astype(F32)).astype(BF16)
        scale_ref[rows, :] = jnp.broadcast_to(scale, (height, LANES))

    moves[2].wait()
    member = facts_ref[0:IMAGES, :].astype(BF16)
    sizes = facts_ref[2 * IMAGES :, :][:, :1]
    pooled = jnp.dot(member, rows_ref[0:SLOTS, :], preferred_element_type=F32)
    pooled = pooled + jnp.dot(member, normed_low[...], preferred_element_type=F32)
    pooled = pooled / sizes
    embed_norm = jnp.sqrt(jnp.sum(pooled * pooled, axis=1, keepdims=True) + 1e-06)
    embedding = pooled / embed_norm
    embed_b = embedding.astype(BF16)
    moves[3].wait()
    moves[4].wait()
    texts = texts_ref[...]
    logits = LOGIT_SCALE_TEMP * lax.dot_general(
        embed_b, texts, (((1,), (1,)), ((), ())), preferred_element_type=F32
    ) + LOGIT_BIAS_SHIFT
    positive = facts_ref[IMAGES : 2 * IMAGES, :]
    sigmoid = 1.0 / (1.0 + jnp.exp(-logits))
    weights = (LOSS_SCALE_FACTOR * LOGIT_SCALE_TEMP * (sigmoid - positive)).astype(BF16)
    embed_grad = jnp.dot(weights, texts, preferred_element_type=F32)
    radial = jnp.sum(embedding * embed_grad, axis=1, keepdims=True)
    spread = (embed_grad - embedding * radial) / embed_norm / sizes
    spread = spread - jnp.sum(spread, axis=1, keepdims=True) * (1.0 / D)
    for piece in range(3):
        top = spread.astype(BF16)
        spread_ref[piece * IMAGES : (piece + 1) * IMAGES, :] = top
        spread = spread - top.astype(F32)

    moves[5].wait()

    for at in range(SLOTS // height):
        rows = pl.ds(at * height, height)
        grad = jnp.dot(member3_ref[rows, :], spread_ref[...], preferred_element_type=F32)
        normed = summed[rows, :]
        mean_cross = jnp.sum(grad * normed, axis=1, keepdims=True) * (1.0 / D)
        scale = scale_ref[rows, :][:, :1]
        patches_ref[rows, :] = ((grad - normed * mean_cross) * scale).astype(BF16)

    out = pltpu.make_async_copy(patches_ref, patches_hbm, sems.at[7])
    out.start()
    moves[6].wait()
    packed = jnp.dot(to_message_ref[...], patches_ref[...], preferred_element_type=F32).astype(BF16)
    put_message(send_ref, packed[:WIDE, :], packed[WIDE:, :])
    out.wait()


def slots(arrived, patch_input, half, other, to_slots, to_message, facts, member3):
    return pl.pallas_call(
        slot_kernel,
        in_specs=vmem(1) + any_space(7),
        out_specs=any_space(1) + vmem(1),
        out_shape=[
            jax.ShapeDtypeStruct((SLOTS, D), BF16),
            jax.ShapeDtypeStruct((BLK, MSG, LANES), BF16),
        ],
        scratch_shapes=[
            pltpu.VMEM((SLOTS, D), BF16),
            pltpu.VMEM((SLOTS, D), BF16),
            pltpu.VMEM((SLOTS, SLOT_K), BF16),
            pltpu.VMEM((WIDE + BLK, SLOTS), BF16),
            pltpu.VMEM((3 * IMAGES, SLOTS), F32),
            pltpu.VMEM((SLOTS, 3 * IMAGES), BF16),
            pltpu.VMEM((SLOTS, D), BF16),
            pltpu.VMEM((SLOT_K, D), BF16),
            pltpu.VMEM((SLOTS, D), F32),
            pltpu.VMEM((SLOTS, D), BF16),
            pltpu.VMEM((SLOTS, LANES), F32),
            pltpu.VMEM((3 * IMAGES, D), BF16),
            pltpu.SemaphoreType.DMA((8,)),
        ],
        compiler_params=params(28),
        cost_estimate=pl.CostEstimate(
            flops=40 * SLOTS * SLOT_K * D, bytes_accessed=100 * 2**20, transcendentals=IMAGES * SLOTS
        ),
        name="slot_gradients",
    )(arrived, *(pltpu.with_memory_space_constraint(a, pltpu.HBM) for a in (
        patch_input, half, other, to_slots, to_message, facts, member3
    )))


def slope(entries):
    square = entries * entries
    tangent = jnp.tanh(GELU_A * (entries + GELU_B * square * entries))
    return 0.5 * (1.0 + tangent) + 0.5 * entries * (1.0 - tangent * tangent) * GELU_A * (
        1.0 + 3.0 * GELU_B * square
    )


def backward_kernel(
    arrived_ref, to_rows_ref, hidden_ref, weight_ref, out_ref, out_buf, rows_ref, sems
):
    take_message(arrived_ref, rows_ref)
    grads = jnp.dot(to_rows_ref[...], rows_ref[...], preferred_element_type=F32).astype(BF16)
    rows_ref[0:ROWS, :] = grads
    copies = []
    for k in range(CHUNKS):
        part = slice(k * CHUNK, (k + 1) * CHUNK)
        active_grad = lax.dot_general(
            rows_ref[0:ROWS, :], weight_ref[part, :], (((1,), (1,)), ((), ())),
            preferred_element_type=F32,
        )
        out_buf[:, part] = (slope(hidden_ref[:, part].astype(F32)) * active_grad).astype(BF16)
        copy = pltpu.make_async_copy(out_buf.at[:, part], out_ref.at[:, part], sems.at[k])
        copy.start()
        copies.append(copy)
    for copy in copies:
        copy.wait()


def backward(arrived, to_rows, hidden, weight):
    return pl.pallas_call(
        backward_kernel,
        in_specs=vmem(4),
        out_specs=pl.BlockSpec(memory_space=pl.ANY),
        out_shape=jax.ShapeDtypeStruct((ROWS, FF), BF16),
        scratch_shapes=[
            pltpu.VMEM((ROWS, FF), BF16),
            pltpu.VMEM((SLOT_K, D), BF16),
            pltpu.SemaphoreType.DMA((CHUNKS,)),
        ],
        compiler_params=params(26),
        cost_estimate=pl.CostEstimate(
            flops=2 * ROWS * FF * D, bytes_accessed=2 * (FF * D + 2 * ROWS * FF), transcendentals=ROWS * FF
        ),
        name="owner_backward",
    )(arrived, to_rows, hidden, weight)


def on_device(
    patch_input, hidden_pre, down_weight, text_features, patch_counts, owners, pair_labels
):
    position = lax.axis_index("blk")
    place = lax.axis_index("grp")
    grp_count = lax.axis_size("grp")
    tallies = tally(owners)
    text, tallies = lax.optimization_barrier((text_features, tallies))
    met = [text]
    for distance in range(1, STEPS):
        route = [((i - distance) % BLK, i) for i in range(BLK)]
        met.append(lax.ppermute(text, "blk", route))
    branch = forward(hidden_pre, down_weight)
    branch, position, place, *met = lax.optimization_barrier((branch, position, place, *met))
    near = jnp.concatenate(met, axis=0)
    near, tallies = lax.optimization_barrier((near, tallies))

    def swapped(block, masks):
        return lax.ppermute(block, "grp", [(i, i ^ masks[i % 2]) for i in range(grp_count)])

    first = swapped(near, (2, 6))
    second = swapped(near, (6, 2))
    counts = lax.all_to_all(tallies, "blk", split_axis=0, concat_axis=0, tiled=True)
    first, second = lax.optimization_barrier((first, second))
    third = swapped(first, (6, 2))
    message = pack(counts, branch)
    ring = (near, first, second, third)
    message, owners, patch_counts, pair_labels, *ring = lax.optimization_barrier(
        (message, owners, patch_counts, pair_labels, *ring)
    )
    arrived = lax.all_to_all(message, "blk", split_axis=0, concat_axis=0, tiled=True)

    half = normalised(ring)
    other = lax.ppermute(half, "grp", [(i, i ^ 1) for i in range(grp_count)])
    at = jnp.arange(grp_count * STEPS * IMAGES, dtype=I32)
    source = (position - (at // IMAGES) % STEPS) % BLK
    hop = at // (STEPS * IMAGES) % STEPS
    holder = jnp.where(at < STEPS * STEPS * IMAGES, place, place ^ 1)
    near_mask = jnp.where(holder % 2 == 0, 2, 6)
    mask = jnp.where(hop == 1, near_mask, jnp.where(hop == 2, 8 - near_mask, 4 * (hop // 3)))
    device = holder ^ mask
    columns = source * (grp_count * IMAGES) + device * IMAGES + at % IMAGES

    to_slots, to_message, to_rows, facts, member3 = prepare(
        owners, patch_counts, counts, pair_labels, columns
    )
    d_patches, outgoing = slots(
        arrived, patch_input, half, other, to_slots, to_message, facts, member3
    )
    returned = lax.all_to_all(outgoing, "blk", split_axis=0, concat_axis=0, tiled=True)
    d_hidden = backward(returned, to_rows, hidden_pre, down_weight)
    return (d_patches, d_hidden)


def solution(mesh):
    rows = P(("blk", "grp"), None)
    flat = P(("blk", "grp"))
    return jax.shard_map(
        on_device,
        mesh=mesh,
        in_specs=(rows, rows, P(), rows, flat, flat, flat),
        out_specs=(rows, rows),
        check_vma=False,
    )
```

```python
import jax
import jax.numpy as jnp
from jax import lax
from jax.experimental import pallas as pl
from jax.experimental.pallas import tpu as pltpu
from jax.sharding import PartitionSpec as P

STEPS = 4
GELU_A = 0.7978845608028654
GELU_B = 0.044715
LOGIT_SCALE_TEMP = 10.0
LOGIT_BIAS_SHIFT = -2.0
LOSS_SCALE_FACTOR = 128.0

BLK = 32
CAP = 16
D = 1536
FF = 3072
SLOTS = 512
ROWS = 288
IMAGES = 16
LANES = 128
TILES = D // LANES
MSG = (TILES + 1) * CAP
WIDE = BLK * CAP
CHUNK = 512
CHUNKS = FF // CHUNK
PART = 512
PARTS = D // PART
SLOT_K = 640
F32 = jnp.float32
BF16 = jnp.bfloat16
I32 = jnp.int32


def iota(shape, axis):
    return lax.broadcasted_iota(I32, shape, axis)


def vmem(count):
    return [pl.BlockSpec(memory_space=pltpu.VMEM)] * count


def params(mib):
    return pltpu.CompilerParams(vmem_limit_bytes=mib * 2**20)


def put_rows(send_ref, part, wide):
    for tile in range(PART // LANES):
        start = (part * (PART // LANES) + tile) * CAP
        send_ref[:, start : start + CAP, :] = wide[
            :, tile * LANES : (tile + 1) * LANES
        ].reshape(BLK, CAP, LANES)


def put_extra(send_ref, extra):
    last = extra.reshape(BLK, TILES, LANES)
    last = jnp.concatenate([last, jnp.zeros((BLK, CAP - TILES, LANES), F32)], axis=1)
    send_ref[:, TILES * CAP :, :] = last.astype(BF16)


def take_message(arrived_ref, rows_ref):
    for tile in range(TILES):
        rows_ref[0:WIDE, tile * LANES : (tile + 1) * LANES] = arrived_ref[
            :, tile * CAP : (tile + 1) * CAP, :
        ].reshape(WIDE, LANES)
    last = arrived_ref[:, TILES * CAP :, :].astype(F32)[:, :TILES, :]
    rows_ref[WIDE : WIDE + BLK, :] = last.reshape(BLK, D).astype(BF16)
    rows_ref[WIDE + BLK :, :] = jnp.zeros((SLOT_K - WIDE - BLK, D), BF16)


def starts_of(counts):
    before = (iota((BLK, BLK), 0) > iota((BLK, BLK), 1)).astype(F32).astype(BF16)
    return jnp.dot(before, counts.astype(BF16), preferred_element_type=F32)


def tally_kernel(owners_ref, tallies_ref):
    hits = (owners_ref[...] == iota((BLK, SLOTS), 0)).astype(I32)
    tallies_ref[...] = jnp.broadcast_to(jnp.sum(hits, axis=1, keepdims=True), (BLK, LANES))


def tally(owners):
    return pl.pallas_call(
        tally_kernel,
        in_specs=vmem(1),
        out_specs=pl.BlockSpec(memory_space=pltpu.VMEM),
        out_shape=jax.ShapeDtypeStruct((BLK, LANES), I32),
        compiler_params=params(2),
        cost_estimate=pl.CostEstimate(flops=10**10, bytes_accessed=2**15, transcendentals=0),
        name="tally_owners",
    )(owners[None, :])


def gelu(entries):
    inside = GELU_A * (entries + GELU_B * entries * entries * entries)
    return 0.5 * entries * (1.0 + jnp.tanh(inside))


def forward_kernel(hidden_ref, weight_ref, branch_ref, active, total):
    hidden_buf, weight_buf = hidden_ref, weight_ref

    def activate(k):
        part = slice(k * CHUNK, (k + 1) * CHUNK)
        active[:, part] = gelu(hidden_buf[:, part].astype(F32)).astype(BF16)

    activate(0)
    for k in range(CHUNKS):
        if k + 1 < CHUNKS:
            activate(k + 1)
        part = slice(k * CHUNK, (k + 1) * CHUNK)
        product = jnp.dot(active[:, part], weight_buf[part, :], preferred_element_type=F32)
        if k == 0:
            total[...] = product
        else:
            total[...] += product

    branch_ref[...] = total[...].astype(BF16)


def pack_kernel(counts_ref, branch_ref, send_ref, buffer, sems):
    counts = counts_ref[...].astype(F32)
    starts = starts_of(counts)
    counts_wide = jnp.broadcast_to(counts[:, None, :], (BLK, CAP, LANES)).reshape(WIDE, LANES)[:, :1]
    starts_wide = jnp.broadcast_to(starts[:, None, :], (BLK, CAP, LANES)).reshape(WIDE, LANES)[:, :1]
    rank = (iota((WIDE, 1), 0) & 15).astype(F32)
    key = jnp.where(rank < counts_wide, starts_wide + rank, -1.0)
    pick = (iota((WIDE, ROWS), 1).astype(F32) == key).astype(F32).astype(BF16)
    extra_key = jnp.where(counts[:, :1] > CAP, starts[:, :1] + CAP, -1.0)
    extra_pick = (iota((BLK, ROWS), 1).astype(F32) == extra_key).astype(F32).astype(BF16)
    put_extra(buffer, jnp.dot(extra_pick, branch_ref[...], preferred_element_type=F32))
    copies = []
    begin = 0
    for part in range(PARTS):
        columns = slice(part * PART, (part + 1) * PART)
        wide = jnp.dot(pick, branch_ref[:, columns], preferred_element_type=F32).astype(BF16)
        put_rows(buffer, part, wide)
        end = (part + 1) * (PART // LANES) * CAP if part + 1 < PARTS else MSG
        copy = pltpu.make_async_copy(
            buffer.at[:, begin:end, :], send_ref.at[:, begin:end, :], sems.at[part]
        )
        copy.start()
        copies.append(copy)
        begin = end
    for copy in copies:
        copy.wait()


def any_space(count):
    return [pl.BlockSpec(memory_space=pltpu.HBM)] * count


def forward(hidden, weight):
    return pl.pallas_call(
        forward_kernel,
        in_specs=vmem(2),
        out_specs=pl.BlockSpec(memory_space=pltpu.VMEM),
        out_shape=jax.ShapeDtypeStruct((ROWS, D), BF16),
        scratch_shapes=[pltpu.VMEM((ROWS, FF), BF16), pltpu.VMEM((ROWS, D), F32)],
        compiler_params=params(24),
        cost_estimate=pl.CostEstimate(
            flops=2 * ROWS * FF * D, bytes_accessed=2 * (FF * D + ROWS * FF), transcendentals=ROWS * FF
        ),
        name="owner_forward",
    )(hidden, weight)


def pack(counts, branch):
    return pl.pallas_call(
        pack_kernel,
        in_specs=vmem(2),
        out_specs=pl.BlockSpec(memory_space=pltpu.HBM),
        scratch_shapes=[pltpu.VMEM((BLK, MSG, LANES), BF16), pltpu.SemaphoreType.DMA((PARTS,))],
        out_shape=pltpu.HBM((BLK, MSG, LANES), BF16),
        compiler_params=params(16),
        cost_estimate=pl.CostEstimate(
            flops=3 * 10**9, bytes_accessed=2**12, transcendentals=0
        ),
        name="owner_pack",
    )(counts, branch)


def texts_kernel(near_ref, first_ref, second_ref, third_ref, texts_ref):
    height = STEPS * IMAGES
    for at, ref in enumerate((near_ref, first_ref, second_ref, third_ref)):
        text = ref[...].astype(F32)
        norm = jnp.sqrt(jnp.sum(text * text, axis=1, keepdims=True) + 1e-06)
        texts_ref[at * height : (at + 1) * height, :] = (text / norm).astype(BF16)


def normalised(ring):
    return pl.pallas_call(
        texts_kernel,
        in_specs=vmem(4),
        out_specs=pl.BlockSpec(memory_space=pltpu.VMEM),
        out_shape=pltpu.HBM((STEPS * STEPS * IMAGES, D), BF16),
        compiler_params=params(12),
        cost_estimate=pl.CostEstimate(flops=1, bytes_accessed=2**20, transcendentals=0),
        name="normalise_texts",
    )(*ring)


def prepare_kernel(
    owners_row_ref, owners_col_ref, sizes_row_ref, sizes_col_ref, counts_ref, labels_ref, columns_ref,
    to_slots_ref, to_message_ref, to_rows_ref, facts_ref, member3_ref,
):
    owners = owners_col_ref[...]
    hits = owners == iota((SLOTS, BLK), 1)
    earlier = (iota((SLOTS, SLOTS), 0) > iota((SLOTS, SLOTS), 1)).astype(F32).astype(BF16)
    prefix = jnp.dot(earlier, hits.astype(F32).astype(BF16), preferred_element_type=F32)
    rank = jnp.sum(jnp.where(hits, prefix, 0.0), axis=1, keepdims=True).astype(I32)
    place = jnp.where(rank < CAP, owners * CAP + rank, WIDE + owners)
    place = jnp.where(owners >= 0, place, -1)
    to_slots_ref[...] = (iota((SLOTS, SLOT_K), 1) == place).astype(F32).astype(BF16)

    owners = owners_row_ref[...]
    hits = owners == iota((BLK, SLOTS), 0)
    earlier = (iota((SLOTS, SLOTS), 0) < iota((SLOTS, SLOTS), 1)).astype(F32).astype(BF16)
    prefix = jnp.dot(hits.astype(F32).astype(BF16), earlier, preferred_element_type=F32)
    rank = jnp.sum(jnp.where(hits, prefix, 0.0), axis=0, keepdims=True).astype(I32)
    place = jnp.where(rank < CAP, owners * CAP + rank, WIDE + owners)
    place = jnp.where(owners >= 0, place, -1)
    to_message_ref[...] = (iota((WIDE + BLK, SLOTS), 0) == place).astype(F32).astype(BF16)

    counts = counts_ref[...].astype(F32)
    starts = starts_of(counts)
    own = iota((BLK, SLOT_K), 0)
    lane = iota((BLK, SLOT_K), 1)
    extra = lane >= WIDE
    mine = jnp.where(extra, lane - WIDE, lane >> 4) == own
    rank = jnp.where(extra, CAP, lane & 15).astype(F32)
    valid = mine & (rank < counts[:, :1])
    key = jnp.sum(jnp.where(valid, starts[:, :1] + rank + 1.0, 0.0), axis=0, keepdims=True) - 1.0
    to_rows_ref[...] = (iota((ROWS, SLOT_K), 0).astype(F32) == key).astype(F32).astype(BF16)

    sizes_row = sizes_row_ref[...].astype(F32)
    sizes_col = sizes_col_ref[...].astype(F32)
    row = iota((IMAGES, IMAGES), 0)
    column = iota((IMAGES, IMAGES), 1)
    begin = jnp.sum(jnp.where(column < row, sizes_row, 0.0), axis=1, keepdims=True)
    slot = iota((IMAGES, SLOTS), 1).astype(F32)
    facts_ref[0:IMAGES, :] = ((slot >= begin) & (slot < begin + sizes_col)).astype(F32)
    facts_ref[IMAGES : 2 * IMAGES, :] = (labels_ref[...] == columns_ref[...]).astype(F32)
    facts_ref[2 * IMAGES :, :] = jnp.broadcast_to(sizes_col, (IMAGES, SLOTS))
    begin = jnp.sum(jnp.where(row < column, sizes_col, 0.0), axis=0, keepdims=True)
    slot = iota((SLOTS, IMAGES), 0).astype(F32)
    member = ((slot >= begin) & (slot < begin + sizes_row)).astype(F32)
    member3_ref[...] = jnp.concatenate([member, member, member], axis=1).astype(BF16)


def prepare(owners, patch_counts, counts, labels, columns):
    shapes = (
        (SLOTS, SLOT_K), (WIDE + BLK, SLOTS), (ROWS, SLOT_K), (3 * IMAGES, SLOTS), (SLOTS, 3 * IMAGES),
    )
    return pl.pallas_call(
        prepare_kernel,
        in_specs=vmem(7),
        out_specs=vmem(5),
        out_shape=[pltpu.HBM(shape, F32 if at == 3 else BF16) for at, shape in enumerate(shapes)],
        compiler_params=params(24),
        cost_estimate=pl.CostEstimate(flops=100*10**9, bytes_accessed=2**12, transcendentals=0),
        name="prepare_onehots",
    )(owners[None, :], owners[:, None], patch_counts[None, :], patch_counts[:, None], counts,
      labels[:, None], columns[None, :])


def slot_kernel(
    arrived_ref, patch_hbm, half_hbm, other_hbm, to_slots_hbm, to_message_hbm, facts_hbm, member3_hbm, weight_hbm,
    patches_hbm, send_ref, weight_ref,
    patch_ref, texts_ref, to_slots_ref, to_message_ref, facts_ref, member3_ref,
    patches_ref, rows_ref, summed, normed_low, scale_ref, spread_ref, sems,
):
    moves = [
        pltpu.make_async_copy(source, target, sems.at[at])
        for at, (source, target) in enumerate((
            (to_slots_hbm, to_slots_ref), (patch_hbm, patch_ref),
            (facts_hbm, facts_ref), (half_hbm, texts_ref.at[: SLOTS // 2, :]),
            (other_hbm, texts_ref.at[SLOTS // 2 :, :]),
            (member3_hbm, member3_ref), (to_message_hbm, to_message_ref),
        ))
    ]
    for copy in moves:
        copy.start()
    take_message(arrived_ref, rows_ref)
    moves[0].wait()
    to_slots = to_slots_ref[...]
    width = 512
    for part in range(D // width):
        columns = slice(part * width, (part + 1) * width)
        summed[:, columns] = jnp.dot(to_slots, rows_ref[:, columns], preferred_element_type=F32)

    height = 128
    moves[1].wait()
    weight_copy = pltpu.make_async_copy(weight_hbm, weight_ref, sems.at[8])
    weight_copy.start()

    for at in range(SLOTS // height):
        rows = pl.ds(at * height, height)
        values = summed[rows, :] + patch_ref[rows, :].astype(F32)
        centered = values - jnp.sum(values, axis=1, keepdims=True) * (1.0 / D)
        variance = jnp.sum(centered * centered, axis=1, keepdims=True) * (1.0 / D)
        scale = lax.rsqrt(variance + 1e-06)
        normed = centered * scale
        summed[rows, :] = normed
        high = normed.astype(BF16)
        rows_ref[rows, :] = high
        normed_low[rows, :] = (normed - high.astype(F32)).astype(BF16)
        scale_ref[rows, :] = jnp.broadcast_to(scale, (height, LANES))

    moves[2].wait()
    member = facts_ref[0:IMAGES, :].astype(BF16)
    sizes = facts_ref[2 * IMAGES :, :][:, :1]
    pooled = jnp.dot(member, rows_ref[0:SLOTS, :], preferred_element_type=F32)
    pooled = pooled + jnp.dot(member, normed_low[...], preferred_element_type=F32)
    pooled = pooled / sizes
    embed_norm = jnp.sqrt(jnp.sum(pooled * pooled, axis=1, keepdims=True) + 1e-06)
    embedding = pooled / embed_norm
    embed_b = embedding.astype(BF16)
    moves[3].wait()
    moves[4].wait()
    texts = texts_ref[...]
    logits = LOGIT_SCALE_TEMP * lax.dot_general(
        embed_b, texts, (((1,), (1,)), ((), ())), preferred_element_type=F32
    ) + LOGIT_BIAS_SHIFT
    positive = facts_ref[IMAGES : 2 * IMAGES, :]
    sigmoid = 1.0 / (1.0 + jnp.exp(-logits))
    weights = (LOSS_SCALE_FACTOR * LOGIT_SCALE_TEMP * (sigmoid - positive)).astype(BF16)
    embed_grad = jnp.dot(weights, texts, preferred_element_type=F32)
    radial = jnp.sum(embedding * embed_grad, axis=1, keepdims=True)
    spread = (embed_grad - embedding * radial) / embed_norm / sizes
    spread = spread - jnp.sum(spread, axis=1, keepdims=True) * (1.0 / D)
    for piece in range(3):
        top = spread.astype(BF16)
        spread_ref[piece * IMAGES : (piece + 1) * IMAGES, :] = top
        spread = spread - top.astype(F32)

    moves[5].wait()

    for at in range(SLOTS // height):
        rows = pl.ds(at * height, height)
        grad = jnp.dot(member3_ref[rows, :], spread_ref[...], preferred_element_type=F32)
        normed = summed[rows, :]
        mean_cross = jnp.sum(grad * normed, axis=1, keepdims=True) * (1.0 / D)
        scale = scale_ref[rows, :][:, :1]
        patches_ref[rows, :] = ((grad - normed * mean_cross) * scale).astype(BF16)

    out = pltpu.make_async_copy(patches_ref, patches_hbm, sems.at[7])
    out.start()
    moves[6].wait()
    put_extra(send_ref, jnp.dot(to_message_ref[WIDE:, :], patches_ref[...], preferred_element_type=F32))
    for part in range(PARTS):
        wide = jnp.dot(
            to_message_ref[:WIDE, :], patches_ref[:, part * PART : (part + 1) * PART],
            preferred_element_type=F32,
        )
        put_rows(send_ref, part, wide.astype(BF16))
    out.wait()
    weight_copy.wait()


def slots(arrived, patch_input, half, other, to_slots, to_message, facts, member3, weight):
    return pl.pallas_call(
        slot_kernel,
        in_specs=vmem(1) + any_space(8),
        out_specs=any_space(1) + vmem(2),
        out_shape=[
            jax.ShapeDtypeStruct((SLOTS, D), BF16),
            jax.ShapeDtypeStruct((BLK, MSG, LANES), BF16),
            pltpu.VMEM((FF, D), BF16),
        ],
        scratch_shapes=[
            pltpu.VMEM((SLOTS, D), BF16),
            pltpu.VMEM((SLOTS, D), BF16),
            pltpu.VMEM((SLOTS, SLOT_K), BF16),
            pltpu.VMEM((WIDE + BLK, SLOTS), BF16),
            pltpu.VMEM((3 * IMAGES, SLOTS), F32),
            pltpu.VMEM((SLOTS, 3 * IMAGES), BF16),
            pltpu.VMEM((SLOTS, D), BF16),
            pltpu.VMEM((SLOT_K, D), BF16),
            pltpu.VMEM((SLOTS, D), F32),
            pltpu.VMEM((SLOTS, D), BF16),
            pltpu.VMEM((SLOTS, LANES), F32),
            pltpu.VMEM((3 * IMAGES, D), BF16),
            pltpu.SemaphoreType.DMA((9,)),
        ],
        compiler_params=params(28),
        cost_estimate=pl.CostEstimate(
            flops=4 * SLOTS * SLOT_K * D, bytes_accessed=10 * 2**20, transcendentals=IMAGES * SLOTS
        ),
        name="slot_gradients",
    )(arrived, *(pltpu.with_memory_space_constraint(a, pltpu.HBM) for a in (
        patch_input, half, other, to_slots, to_message, facts, member3, weight
    )))


def slope(entries):
    square = entries * entries
    half = 0.5 * jnp.tanh(entries * (GELU_A + GELU_A * GELU_B * square)) + 0.5
    rise = entries * (2.0 * GELU_A + 6.0 * GELU_A * GELU_B * square)
    return half + half * (1.0 - half) * rise


def backward_kernel(
    arrived_ref, to_rows_ref, hidden_ref, weight_ref, out_ref, out_buf, rows_ref, sems
):
    take_message(arrived_ref, rows_ref)
    grads = jnp.dot(to_rows_ref[...], rows_ref[...], preferred_element_type=F32).astype(BF16)
    rows_ref[0:ROWS, :] = grads
    copies = []
    for k in range(CHUNKS):
        part = slice(k * CHUNK, (k + 1) * CHUNK)
        active_grad = lax.dot_general(
            rows_ref[0:ROWS, :], weight_ref[part, :], (((1,), (1,)), ((), ())),
            preferred_element_type=F32,
        )
        out_buf[:, part] = (slope(hidden_ref[:, part].astype(F32)) * active_grad).astype(BF16)
        copy = pltpu.make_async_copy(out_buf.at[:, part], out_ref.at[:, part], sems.at[k])
        copy.start()
        copies.append(copy)
    for copy in copies:
        copy.wait()


def backward(arrived, to_rows, hidden, weight):
    return pl.pallas_call(
        backward_kernel,
        in_specs=vmem(4),
        out_specs=pl.BlockSpec(memory_space=pl.ANY),
        out_shape=jax.ShapeDtypeStruct((ROWS, FF), BF16),
        scratch_shapes=[
            pltpu.VMEM((ROWS, FF), BF16),
            pltpu.VMEM((SLOT_K, D), BF16),
            pltpu.SemaphoreType.DMA((CHUNKS,)),
        ],
        compiler_params=params(26),
        cost_estimate=pl.CostEstimate(
            flops=2 * ROWS * FF * D, bytes_accessed=2 * (FF * D + 2 * ROWS * FF), transcendentals=ROWS * FF
        ),
        name="owner_backward",
    )(arrived, to_rows, hidden, weight)


def on_device(
    patch_input, hidden_pre, down_weight, text_features, patch_counts, owners, pair_labels
):
    position = lax.axis_index("blk")
    place = lax.axis_index("grp")
    grp_count = lax.axis_size("grp")
    tallies = tally(owners)
    text, tallies = lax.optimization_barrier((text_features, tallies))
    met = [text]
    for distance in range(1, STEPS):
        route = [((i - distance) % BLK, i) for i in range(BLK)]
        met.append(lax.ppermute(text, "blk", route))
    branch = forward(hidden_pre, down_weight)
    branch, position, place, *met = lax.optimization_barrier((branch, position, place, *met))
    near = jnp.concatenate(met, axis=0)
    near, tallies = lax.optimization_barrier((near, tallies))

    def swapped(block, masks):
        return lax.ppermute(block, "grp", [(i, i ^ masks[i % 2]) for i in range(grp_count)])

    first = swapped(near, (2, 6))
    second = swapped(near, (6, 2))
    counts = lax.all_to_all(tallies, "blk", split_axis=0, concat_axis=0, tiled=True)
    first, second = lax.optimization_barrier((first, second))
    third = swapped(first, (6, 2))
    message = pack(counts, branch)
    message, owners, patch_counts, pair_labels, near, first, second = lax.optimization_barrier(
        (message, owners, patch_counts, pair_labels, near, first, second)
    )
    ring = (near, first, second, third)
    arrived = lax.all_to_all(message, "blk", split_axis=0, concat_axis=0, tiled=True)

    half = normalised(ring)
    other = lax.ppermute(half, "grp", [(i, i ^ 1) for i in range(grp_count)])
    at = jnp.arange(grp_count * STEPS * IMAGES, dtype=I32)
    source = (position - (at // IMAGES) % STEPS) % BLK
    hop = at // (STEPS * IMAGES) % STEPS
    holder = jnp.where(at < STEPS * STEPS * IMAGES, place, place ^ 1)
    near_mask = jnp.where(holder % 2 == 0, 2, 6)
    mask = jnp.where(hop == 1, near_mask, jnp.where(hop == 2, 8 - near_mask, 4 * (hop // 3)))
    device = holder ^ mask
    columns = source * (grp_count * IMAGES) + device * IMAGES + at % IMAGES

    to_slots, to_message, to_rows, facts, member3 = prepare(
        owners, patch_counts, counts, pair_labels, columns
    )
    d_patches, outgoing, weight_near = slots(
        arrived, patch_input, half, other, to_slots, to_message, facts, member3, down_weight
    )
    returned = lax.all_to_all(outgoing, "blk", split_axis=0, concat_axis=0, tiled=True)
    d_hidden = backward(returned, to_rows, hidden_pre, weight_near)
    return (d_patches, d_hidden)


def solution(mesh):
    rows = P(("blk", "grp"), None)
    flat = P(("blk", "grp"))
    return jax.shard_map(
        on_device,
        mesh=mesh,
        in_specs=(rows, rows, P(), rows, flat, flat, flat),
        out_specs=(rows, rows),
        check_vma=False,
    )
```

```python
import jax
import jax.numpy as jnp
from jax import lax
from jax.experimental import pallas as pl
from jax.experimental.pallas import tpu as pltpu
from jax.sharding import PartitionSpec as P

STEPS = 4
GELU_A = 0.7978845608028654
GELU_B = 0.044715
LOGIT_SCALE_TEMP = 10.0
LOGIT_BIAS_SHIFT = -2.0
LOSS_SCALE_FACTOR = 128.0

BLK = 32
CAP = 16
D = 1536
FF = 3072
SLOTS = 512
ROWS = 288
IMAGES = 16
LANES = 128
TILES = D // LANES
MSG = (TILES + 1) * CAP
WIDE = BLK * CAP
CHUNK = 512
CHUNKS = FF // CHUNK
PART = 512
PARTS = D // PART
SLOT_K = 640
F32 = jnp.float32
BF16 = jnp.bfloat16
I32 = jnp.int32


def iota(shape, axis):
    return lax.broadcasted_iota(I32, shape, axis)


def vmem(count):
    return [pl.BlockSpec(memory_space=pltpu.VMEM)] * count


def params(mib):
    return pltpu.CompilerParams(vmem_limit_bytes=mib * 2**20)


def put_rows(send_ref, part, wide):
    for tile in range(PART // LANES):
        start = (part * (PART // LANES) + tile) * CAP
        send_ref[:, start : start + CAP, :] = wide[
            :, tile * LANES : (tile + 1) * LANES
        ].reshape(BLK, CAP, LANES)


def put_extra(send_ref, extra):
    last = extra.reshape(BLK, TILES, LANES)
    last = jnp.concatenate([last, jnp.zeros((BLK, CAP - TILES, LANES), F32)], axis=1)
    send_ref[:, TILES * CAP :, :] = last.astype(BF16)


def take_message(arrived_ref, rows_ref):
    for tile in range(TILES):
        rows_ref[0:WIDE, tile * LANES : (tile + 1) * LANES] = arrived_ref[
            :, tile * CAP : (tile + 1) * CAP, :
        ].reshape(WIDE, LANES)
    last = arrived_ref[:, TILES * CAP :, :].astype(F32)[:, :TILES, :]
    rows_ref[WIDE : WIDE + BLK, :] = last.reshape(BLK, D).astype(BF16)
    rows_ref[WIDE + BLK :, :] = jnp.zeros((SLOT_K - WIDE - BLK, D), BF16)


def starts_of(counts):
    before = (iota((BLK, BLK), 0) > iota((BLK, BLK), 1)).astype(F32).astype(BF16)
    return jnp.dot(before, counts.astype(BF16), preferred_element_type=F32)


def tally_kernel(owners_ref, tallies_ref):
    hits = (owners_ref[...] == iota((BLK, SLOTS), 0)).astype(I32)
    tallies_ref[...] = jnp.broadcast_to(jnp.sum(hits, axis=1, keepdims=True), (BLK, LANES))


def tally(owners):
    return pl.pallas_call(
        tally_kernel,
        in_specs=vmem(1),
        out_specs=pl.BlockSpec(memory_space=pltpu.VMEM),
        out_shape=jax.ShapeDtypeStruct((BLK, LANES), I32),
        compiler_params=params(2),
        cost_estimate=pl.CostEstimate(flops=10**10, bytes_accessed=2**15, transcendentals=0),
        name="tally_owners",
    )(pltpu.with_memory_space_constraint(owners[None, :], pltpu.HBM))


def gelu(entries):
    inside = GELU_A * (entries + GELU_B * entries * entries * entries)
    return 0.5 * entries * (1.0 + jnp.tanh(inside))


def forward_kernel(hidden_ref, weight_ref, branch_ref, active, total):
    hidden_buf, weight_buf = hidden_ref, weight_ref

    def activate(k):
        part = slice(k * CHUNK, (k + 1) * CHUNK)
        active[:, part] = gelu(hidden_buf[:, part].astype(F32)).astype(BF16)

    activate(0)
    for k in range(CHUNKS):
        if k + 1 < CHUNKS:
            activate(k + 1)
        part = slice(k * CHUNK, (k + 1) * CHUNK)
        product = jnp.dot(active[:, part], weight_buf[part, :], preferred_element_type=F32)
        if k == 0:
            total[...] = product
        else:
            total[...] += product

    branch_ref[...] = total[...].astype(BF16)


def pack_kernel(counts_ref, branch_ref, send_ref, buffer, sems):
    counts = counts_ref[...].astype(F32)
    starts = starts_of(counts)
    counts_wide = jnp.broadcast_to(counts[:, None, :], (BLK, CAP, LANES)).reshape(WIDE, LANES)[:, :1]
    starts_wide = jnp.broadcast_to(starts[:, None, :], (BLK, CAP, LANES)).reshape(WIDE, LANES)[:, :1]
    rank = (iota((WIDE, 1), 0) & 15).astype(F32)
    key = jnp.where(rank < counts_wide, starts_wide + rank, -1.0)
    pick = (iota((WIDE, ROWS), 1).astype(F32) == key).astype(F32).astype(BF16)
    extra_key = jnp.where(counts[:, :1] > CAP, starts[:, :1] + CAP, -1.0)
    extra_pick = (iota((BLK, ROWS), 1).astype(F32) == extra_key).astype(F32).astype(BF16)
    put_extra(buffer, jnp.dot(extra_pick, branch_ref[...], preferred_element_type=F32))
    copies = []
    begin = 0
    for part in range(PARTS):
        columns = slice(part * PART, (part + 1) * PART)
        wide = jnp.dot(pick, branch_ref[:, columns], preferred_element_type=F32).astype(BF16)
        put_rows(buffer, part, wide)
        end = (part + 1) * (PART // LANES) * CAP if part + 1 < PARTS else MSG
        copy = pltpu.make_async_copy(
            buffer.at[:, begin:end, :], send_ref.at[:, begin:end, :], sems.at[part]
        )
        copy.start()
        copies.append(copy)
        begin = end
    for copy in copies:
        copy.wait()


def any_space(count):
    return [pl.BlockSpec(memory_space=pltpu.HBM)] * count


def forward(hidden, weight):
    return pl.pallas_call(
        forward_kernel,
        in_specs=vmem(2),
        out_specs=pl.BlockSpec(memory_space=pltpu.VMEM),
        out_shape=jax.ShapeDtypeStruct((ROWS, D), BF16),
        scratch_shapes=[pltpu.VMEM((ROWS, FF), BF16), pltpu.VMEM((ROWS, D), F32)],
        compiler_params=params(24),
        cost_estimate=pl.CostEstimate(
            flops=2 * ROWS * FF * D, bytes_accessed=2 * (FF * D + ROWS * FF), transcendentals=ROWS * FF
        ),
        name="owner_forward",
    )(hidden, weight)


def pack(counts, branch):
    return pl.pallas_call(
        pack_kernel,
        in_specs=vmem(2),
        out_specs=pl.BlockSpec(memory_space=pltpu.HBM),
        scratch_shapes=[pltpu.VMEM((BLK, MSG, LANES), BF16), pltpu.SemaphoreType.DMA((PARTS,))],
        out_shape=pltpu.HBM((BLK, MSG, LANES), BF16),
        compiler_params=params(16),
        cost_estimate=pl.CostEstimate(
            flops=3 * 10**9, bytes_accessed=2**12, transcendentals=0
        ),
        name="owner_pack",
    )(counts, branch)


def texts_kernel(near_ref, first_ref, second_ref, third_ref, texts_ref):
    height = STEPS * IMAGES
    for at, ref in enumerate((near_ref, first_ref, second_ref, third_ref)):
        text = ref[...].astype(F32)
        norm = jnp.sqrt(jnp.sum(text * text, axis=1, keepdims=True) + 1e-06)
        texts_ref[at * height : (at + 1) * height, :] = (text / norm).astype(BF16)


def normalised(ring):
    return pl.pallas_call(
        texts_kernel,
        in_specs=vmem(4),
        out_specs=pl.BlockSpec(memory_space=pltpu.VMEM),
        out_shape=pltpu.HBM((STEPS * STEPS * IMAGES, D), BF16),
        compiler_params=params(12),
        cost_estimate=pl.CostEstimate(flops=1, bytes_accessed=2**20, transcendentals=0),
        name="normalise_texts",
    )(*ring)


def prepare_kernel(
    owners_row_ref, owners_col_ref, sizes_row_ref, sizes_col_ref, counts_ref, labels_ref, columns_ref,
    to_slots_ref, to_message_ref, to_rows_ref, facts_ref, member3_ref,
):
    owners = owners_col_ref[...]
    hits = owners == iota((SLOTS, BLK), 1)
    earlier = (iota((SLOTS, SLOTS), 0) > iota((SLOTS, SLOTS), 1)).astype(F32).astype(BF16)
    prefix = jnp.dot(earlier, hits.astype(F32).astype(BF16), preferred_element_type=F32)
    rank = jnp.sum(jnp.where(hits, prefix, 0.0), axis=1, keepdims=True).astype(I32)
    place = jnp.where(rank < CAP, owners * CAP + rank, WIDE + owners)
    place = jnp.where(owners >= 0, place, -1)
    to_slots_ref[...] = (iota((SLOTS, SLOT_K), 1) == place).astype(F32).astype(BF16)

    owners = owners_row_ref[...]
    hits = owners == iota((BLK, SLOTS), 0)
    earlier = (iota((SLOTS, SLOTS), 0) < iota((SLOTS, SLOTS), 1)).astype(F32).astype(BF16)
    prefix = jnp.dot(hits.astype(F32).astype(BF16), earlier, preferred_element_type=F32)
    rank = jnp.sum(jnp.where(hits, prefix, 0.0), axis=0, keepdims=True).astype(I32)
    place = jnp.where(rank < CAP, owners * CAP + rank, WIDE + owners)
    place = jnp.where(owners >= 0, place, -1)
    to_message_ref[...] = (iota((WIDE + BLK, SLOTS), 0) == place).astype(F32).astype(BF16)

    counts = counts_ref[...].astype(F32)
    starts = starts_of(counts)
    own = iota((BLK, SLOT_K), 0)
    lane = iota((BLK, SLOT_K), 1)
    extra = lane >= WIDE
    mine = jnp.where(extra, lane - WIDE, lane >> 4) == own
    rank = jnp.where(extra, CAP, lane & 15).astype(F32)
    valid = mine & (rank < counts[:, :1])
    key = jnp.sum(jnp.where(valid, starts[:, :1] + rank + 1.0, 0.0), axis=0, keepdims=True) - 1.0
    to_rows_ref[...] = (iota((ROWS, SLOT_K), 0).astype(F32) == key).astype(F32).astype(BF16)

    sizes_row = sizes_row_ref[...].astype(F32)
    sizes_col = sizes_col_ref[...].astype(F32)
    row = iota((IMAGES, IMAGES), 0)
    column = iota((IMAGES, IMAGES), 1)
    begin = jnp.sum(jnp.where(column < row, sizes_row, 0.0), axis=1, keepdims=True)
    slot = iota((IMAGES, SLOTS), 1).astype(F32)
    facts_ref[0:IMAGES, :] = ((slot >= begin) & (slot < begin + sizes_col)).astype(F32)
    facts_ref[IMAGES : 2 * IMAGES, :] = (labels_ref[...] == columns_ref[...]).astype(F32)
    facts_ref[2 * IMAGES :, :] = jnp.broadcast_to(sizes_col, (IMAGES, SLOTS))
    begin = jnp.sum(jnp.where(row < column, sizes_col, 0.0), axis=0, keepdims=True)
    slot = iota((SLOTS, IMAGES), 0).astype(F32)
    member = ((slot >= begin) & (slot < begin + sizes_row)).astype(F32)
    member3_ref[...] = jnp.concatenate([member, member, member], axis=1).astype(BF16)


def prepare(owners, patch_counts, counts, labels, columns):
    shapes = (
        (SLOTS, SLOT_K), (WIDE + BLK, SLOTS), (ROWS, SLOT_K), (3 * IMAGES, SLOTS), (SLOTS, 3 * IMAGES),
    )
    return pl.pallas_call(
        prepare_kernel,
        in_specs=vmem(7),
        out_specs=vmem(5),
        out_shape=[pltpu.HBM(shape, F32 if at == 3 else BF16) for at, shape in enumerate(shapes)],
        compiler_params=params(24),
        cost_estimate=pl.CostEstimate(flops=100*10**9, bytes_accessed=2**12, transcendentals=0),
        name="prepare_onehots",
    )(owners[None, :], owners[:, None], patch_counts[None, :], patch_counts[:, None], counts,
      labels[:, None], columns[None, :])


def slot_kernel(
    arrived_ref, patch_hbm, half_hbm, other_hbm, to_slots_hbm, to_message_hbm, facts_hbm, member3_hbm, weight_hbm,
    patches_hbm, send_ref, weight_ref,
    patch_ref, texts_ref, to_slots_ref, to_message_ref, facts_ref, member3_ref,
    patches_ref, rows_ref, summed, normed_low, scale_ref, spread_ref, sems,
):
    moves = [
        pltpu.make_async_copy(source, target, sems.at[at])
        for at, (source, target) in enumerate((
            (to_slots_hbm, to_slots_ref), (patch_hbm, patch_ref),
            (facts_hbm, facts_ref), (half_hbm, texts_ref.at[: SLOTS // 2, :]),
            (other_hbm, texts_ref.at[SLOTS // 2 :, :]),
            (member3_hbm, member3_ref), (to_message_hbm, to_message_ref),
        ))
    ]
    for copy in moves:
        copy.start()
    take_message(arrived_ref, rows_ref)
    moves[0].wait()
    to_slots = to_slots_ref[...]
    width = 512
    for part in range(D // width):
        columns = slice(part * width, (part + 1) * width)
        summed[:, columns] = jnp.dot(to_slots, rows_ref[:, columns], preferred_element_type=F32)

    height = 128
    moves[1].wait()
    weight_copy = pltpu.make_async_copy(weight_hbm, weight_ref, sems.at[8])
    weight_copy.start()

    for at in range(SLOTS // height):
        rows = pl.ds(at * height, height)
        values = summed[rows, :] + patch_ref[rows, :].astype(F32)
        centered = values - jnp.sum(values, axis=1, keepdims=True) * (1.0 / D)
        variance = jnp.sum(centered * centered, axis=1, keepdims=True) * (1.0 / D)
        scale = lax.rsqrt(variance + 1e-06)
        normed = centered * scale
        summed[rows, :] = normed
        high = normed.astype(BF16)
        rows_ref[rows, :] = high
        normed_low[rows, :] = (normed - high.astype(F32)).astype(BF16)
        scale_ref[rows, :] = jnp.broadcast_to(scale, (height, LANES))

    moves[2].wait()
    member = facts_ref[0:IMAGES, :].astype(BF16)
    sizes = facts_ref[2 * IMAGES :, :][:, :1]
    pooled = jnp.dot(member, rows_ref[0:SLOTS, :], preferred_element_type=F32)
    pooled = pooled + jnp.dot(member, normed_low[...], preferred_element_type=F32)
    pooled = pooled / sizes
    embed_norm = jnp.sqrt(jnp.sum(pooled * pooled, axis=1, keepdims=True) + 1e-06)
    embedding = pooled / embed_norm
    embed_b = embedding.astype(BF16)
    moves[3].wait()
    moves[4].wait()
    texts = texts_ref[...]
    logits = LOGIT_SCALE_TEMP * lax.dot_general(
        embed_b, texts, (((1,), (1,)), ((), ())), preferred_element_type=F32
    ) + LOGIT_BIAS_SHIFT
    positive = facts_ref[IMAGES : 2 * IMAGES, :]
    sigmoid = 1.0 / (1.0 + jnp.exp(-logits))
    weights = (LOSS_SCALE_FACTOR * LOGIT_SCALE_TEMP * (sigmoid - positive)).astype(BF16)
    embed_grad = jnp.dot(weights, texts, preferred_element_type=F32)
    radial = jnp.sum(embedding * embed_grad, axis=1, keepdims=True)
    spread = (embed_grad - embedding * radial) / embed_norm / sizes
    spread = spread - jnp.sum(spread, axis=1, keepdims=True) * (1.0 / D)
    for piece in range(3):
        top = spread.astype(BF16)
        spread_ref[piece * IMAGES : (piece + 1) * IMAGES, :] = top
        spread = spread - top.astype(F32)

    moves[5].wait()

    for at in range(SLOTS // height):
        rows = pl.ds(at * height, height)
        grad = jnp.dot(member3_ref[rows, :], spread_ref[...], preferred_element_type=F32)
        normed = summed[rows, :]
        mean_cross = jnp.sum(grad * normed, axis=1, keepdims=True) * (1.0 / D)
        scale = scale_ref[rows, :][:, :1]
        patches_ref[rows, :] = ((grad - normed * mean_cross) * scale).astype(BF16)

    out = pltpu.make_async_copy(patches_ref, patches_hbm, sems.at[7])
    out.start()
    moves[6].wait()
    put_extra(send_ref, jnp.dot(to_message_ref[WIDE:, :], patches_ref[...], preferred_element_type=F32))
    for part in range(PARTS):
        wide = jnp.dot(
            to_message_ref[:WIDE, :], patches_ref[:, part * PART : (part + 1) * PART],
            preferred_element_type=F32,
        )
        put_rows(send_ref, part, wide.astype(BF16))
    out.wait()
    weight_copy.wait()


def slots(arrived, patch_input, half, other, to_slots, to_message, facts, member3, weight):
    return pl.pallas_call(
        slot_kernel,
        in_specs=vmem(1) + any_space(8),
        out_specs=any_space(1) + vmem(2),
        out_shape=[
            jax.ShapeDtypeStruct((SLOTS, D), BF16),
            jax.ShapeDtypeStruct((BLK, MSG, LANES), BF16),
            pltpu.VMEM((FF, D), BF16),
        ],
        scratch_shapes=[
            pltpu.VMEM((SLOTS, D), BF16),
            pltpu.VMEM((SLOTS, D), BF16),
            pltpu.VMEM((SLOTS, SLOT_K), BF16),
            pltpu.VMEM((WIDE + BLK, SLOTS), BF16),
            pltpu.VMEM((3 * IMAGES, SLOTS), F32),
            pltpu.VMEM((SLOTS, 3 * IMAGES), BF16),
            pltpu.VMEM((SLOTS, D), BF16),
            pltpu.VMEM((SLOT_K, D), BF16),
            pltpu.VMEM((SLOTS, D), F32),
            pltpu.VMEM((SLOTS, D), BF16),
            pltpu.VMEM((SLOTS, LANES), F32),
            pltpu.VMEM((3 * IMAGES, D), BF16),
            pltpu.SemaphoreType.DMA((9,)),
        ],
        compiler_params=params(28),
        cost_estimate=pl.CostEstimate(
            flops=4 * SLOTS * SLOT_K * D, bytes_accessed=10 * 2**20, transcendentals=IMAGES * SLOTS
        ),
        name="slot_gradients",
    )(arrived, *(pltpu.with_memory_space_constraint(a, pltpu.HBM) for a in (
        patch_input, half, other, to_slots, to_message, facts, member3, weight
    )))


def slope(entries):
    square = entries * entries
    half = 0.5 * jnp.tanh(entries * (GELU_A + GELU_A * GELU_B * square)) + 0.5
    rise = entries * (2.0 * GELU_A + 6.0 * GELU_A * GELU_B * square)
    return half + half * (1.0 - half) * rise


def backward_kernel(
    arrived_ref, to_rows_ref, hidden_ref, weight_ref, out_ref, out_buf, rows_ref, sems
):
    take_message(arrived_ref, rows_ref)
    grads = jnp.dot(to_rows_ref[...], rows_ref[...], preferred_element_type=F32).astype(BF16)
    rows_ref[0:ROWS, :] = grads
    copies = []
    for k in range(CHUNKS):
        part = slice(k * CHUNK, (k + 1) * CHUNK)
        active_grad = lax.dot_general(
            rows_ref[0:ROWS, :], weight_ref[part, :], (((1,), (1,)), ((), ())),
            preferred_element_type=F32,
        )
        out_buf[:, part] = (slope(hidden_ref[:, part].astype(F32)) * active_grad).astype(BF16)
        copy = pltpu.make_async_copy(out_buf.at[:, part], out_ref.at[:, part], sems.at[k])
        copy.start()
        copies.append(copy)
    for copy in copies:
        copy.wait()


def backward(arrived, to_rows, hidden, weight):
    return pl.pallas_call(
        backward_kernel,
        in_specs=vmem(4),
        out_specs=pl.BlockSpec(memory_space=pl.ANY),
        out_shape=jax.ShapeDtypeStruct((ROWS, FF), BF16),
        scratch_shapes=[
            pltpu.VMEM((ROWS, FF), BF16),
            pltpu.VMEM((SLOT_K, D), BF16),
            pltpu.SemaphoreType.DMA((CHUNKS,)),
        ],
        compiler_params=params(26),
        cost_estimate=pl.CostEstimate(
            flops=2 * ROWS * FF * D, bytes_accessed=2 * (FF * D + 2 * ROWS * FF), transcendentals=ROWS * FF
        ),
        name="owner_backward",
    )(arrived, to_rows, hidden, weight)


def on_device(
    patch_input, hidden_pre, down_weight, text_features, patch_counts, owners, pair_labels
):
    position = lax.axis_index("blk")
    place = lax.axis_index("grp")
    grp_count = lax.axis_size("grp")
    tallies = tally(owners)
    text, tallies = lax.optimization_barrier((text_features, tallies))
    met = [text]
    for distance in range(1, STEPS):
        route = [((i - distance) % BLK, i) for i in range(BLK)]
        met.append(lax.ppermute(text, "blk", route))
    branch = forward(hidden_pre, down_weight)
    branch, position, place, *met = lax.optimization_barrier((branch, position, place, *met))
    near = jnp.concatenate(met, axis=0)
    near, tallies = lax.optimization_barrier((near, tallies))

    def swapped(block, masks):
        return lax.ppermute(block, "grp", [(i, i ^ masks[i % 2]) for i in range(grp_count)])

    first = swapped(near, (2, 6))
    counts = lax.all_to_all(tallies, "blk", split_axis=0, concat_axis=0, tiled=True)
    third = swapped(first, (6, 2))
    near_again, first = lax.optimization_barrier((near, first))
    second = swapped(near_again, (6, 2))
    message = pack(counts, branch)
    message, owners, patch_counts, pair_labels, near, first = lax.optimization_barrier(
        (message, owners, patch_counts, pair_labels, near, first)
    )
    ring = (near, first, second, third)
    arrived = lax.all_to_all(message, "blk", split_axis=0, concat_axis=0, tiled=True)

    half = normalised(ring)
    other = lax.ppermute(half, "grp", [(i, i ^ 1) for i in range(grp_count)])
    at = jnp.arange(grp_count * STEPS * IMAGES, dtype=I32)
    source = (position - (at // IMAGES) % STEPS) % BLK
    hop = at // (STEPS * IMAGES) % STEPS
    holder = jnp.where(at < STEPS * STEPS * IMAGES, place, place ^ 1)
    near_mask = jnp.where(holder % 2 == 0, 2, 6)
    mask = jnp.where(hop == 1, near_mask, jnp.where(hop == 2, 8 - near_mask, 4 * (hop // 3)))
    device = holder ^ mask
    columns = source * (grp_count * IMAGES) + device * IMAGES + at % IMAGES

    to_slots, to_message, to_rows, facts, member3 = prepare(
        owners, patch_counts, counts, pair_labels, columns
    )
    d_patches, outgoing, weight_near = slots(
        arrived, patch_input, half, other, to_slots, to_message, facts, member3, down_weight
    )
    returned = lax.all_to_all(outgoing, "blk", split_axis=0, concat_axis=0, tiled=True)
    d_hidden = backward(returned, to_rows, hidden_pre, weight_near)
    return (d_patches, d_hidden)


def solution(mesh):
    rows = P(("blk", "grp"), None)
    flat = P(("blk", "grp"))
    return jax.shard_map(
        on_device,
        mesh=mesh,
        in_specs=(rows, rows, P(), rows, flat, flat, flat),
        out_specs=(rows, rows),
        check_vma=False,
    )
```

```python
import jax
import jax.numpy as jnp
from jax import lax
from jax.experimental import pallas as pl
from jax.experimental.pallas import tpu as pltpu
from jax.sharding import PartitionSpec as P

STEPS = 4
GELU_A = 0.7978845608028654
GELU_B = 0.044715
LOGIT_SCALE_TEMP = 10.0
LOGIT_BIAS_SHIFT = -2.0
LOSS_SCALE_FACTOR = 128.0

BLK = 32
CAP = 16
D = 1536
FF = 3072
SLOTS = 512
ROWS = 288
IMAGES = 16
LANES = 128
TILES = D // LANES
MSG = (TILES + 1) * CAP
WIDE = BLK * CAP
CHUNK = 512
CHUNKS = FF // CHUNK
PART = 512
PARTS = D // PART
SLOT_K = 640
F32 = jnp.float32
BF16 = jnp.bfloat16
I32 = jnp.int32


def iota(shape, axis):
    return lax.broadcasted_iota(I32, shape, axis)


def vmem(count):
    return [pl.BlockSpec(memory_space=pltpu.VMEM)] * count


def params(mib):
    return pltpu.CompilerParams(vmem_limit_bytes=mib * 2**20)


def put_rows(send_ref, part, wide):
    for tile in range(PART // LANES):
        start = (part * (PART // LANES) + tile) * CAP
        send_ref[:, start : start + CAP, :] = wide[
            :, tile * LANES : (tile + 1) * LANES
        ].reshape(BLK, CAP, LANES)


def put_extra(send_ref, extra):
    last = extra.reshape(BLK, TILES, LANES)
    last = jnp.concatenate([last, jnp.zeros((BLK, CAP - TILES, LANES), F32)], axis=1)
    send_ref[:, TILES * CAP :, :] = last.astype(BF16)


def take_message(arrived_ref, rows_ref):
    for tile in range(TILES):
        rows_ref[0:WIDE, tile * LANES : (tile + 1) * LANES] = arrived_ref[
            :, tile * CAP : (tile + 1) * CAP, :
        ].reshape(WIDE, LANES)
    last = arrived_ref[:, TILES * CAP :, :].astype(F32)[:, :TILES, :]
    rows_ref[WIDE : WIDE + BLK, :] = last.reshape(BLK, D).astype(BF16)
    rows_ref[WIDE + BLK :, :] = jnp.zeros((SLOT_K - WIDE - BLK, D), BF16)


def starts_of(counts):
    before = (iota((BLK, BLK), 0) > iota((BLK, BLK), 1)).astype(F32).astype(BF16)
    return jnp.dot(before, counts.astype(BF16), preferred_element_type=F32)


def tally_kernel(owners_ref, tallies_ref):
    hits = (owners_ref[...] == iota((BLK, SLOTS), 0)).astype(I32)
    tallies_ref[...] = jnp.broadcast_to(jnp.sum(hits, axis=1, keepdims=True), (BLK, LANES))


def tally(owners):
    return pl.pallas_call(
        tally_kernel,
        in_specs=vmem(1),
        out_specs=pl.BlockSpec(memory_space=pltpu.VMEM),
        out_shape=jax.ShapeDtypeStruct((BLK, LANES), I32),
        compiler_params=params(2),
        cost_estimate=pl.CostEstimate(flops=10**10, bytes_accessed=2**15, transcendentals=0),
        name="tally_owners",
    )(pltpu.with_memory_space_constraint(owners[None, :], pltpu.HBM))


def gelu(entries):
    inside = GELU_A * (entries + GELU_B * entries * entries * entries)
    return 0.5 * entries * (1.0 + jnp.tanh(inside))


def forward_kernel(hidden_ref, weight_ref, branch_ref, active, total):
    hidden_buf, weight_buf = hidden_ref, weight_ref

    def activate(k):
        part = slice(k * CHUNK, (k + 1) * CHUNK)
        active[:, part] = gelu(hidden_buf[:, part].astype(F32)).astype(BF16)

    activate(0)
    for k in range(CHUNKS):
        if k + 1 < CHUNKS:
            activate(k + 1)
        part = slice(k * CHUNK, (k + 1) * CHUNK)
        product = jnp.dot(active[:, part], weight_buf[part, :], preferred_element_type=F32)
        if k == 0:
            total[...] = product
        else:
            total[...] += product

    branch_ref[...] = total[...].astype(BF16)


def pack_kernel(counts_ref, branch_ref, send_ref, buffer, sems):
    counts = counts_ref[...].astype(F32)
    starts = starts_of(counts)
    counts_wide = jnp.broadcast_to(counts[:, None, :], (BLK, CAP, LANES)).reshape(WIDE, LANES)[:, :1]
    starts_wide = jnp.broadcast_to(starts[:, None, :], (BLK, CAP, LANES)).reshape(WIDE, LANES)[:, :1]
    rank = (iota((WIDE, 1), 0) & 15).astype(F32)
    key = jnp.where(rank < counts_wide, starts_wide + rank, -1.0)
    pick = (iota((WIDE, ROWS), 1).astype(F32) == key).astype(F32).astype(BF16)
    extra_key = jnp.where(counts[:, :1] > CAP, starts[:, :1] + CAP, -1.0)
    extra_pick = (iota((BLK, ROWS), 1).astype(F32) == extra_key).astype(F32).astype(BF16)
    put_extra(buffer, jnp.dot(extra_pick, branch_ref[...], preferred_element_type=F32))
    copies = []
    begin = 0
    for part in range(PARTS):
        columns = slice(part * PART, (part + 1) * PART)
        wide = jnp.dot(pick, branch_ref[:, columns], preferred_element_type=F32).astype(BF16)
        put_rows(buffer, part, wide)
        end = (part + 1) * (PART // LANES) * CAP if part + 1 < PARTS else MSG
        copy = pltpu.make_async_copy(
            buffer.at[:, begin:end, :], send_ref.at[:, begin:end, :], sems.at[part]
        )
        copy.start()
        copies.append(copy)
        begin = end
    for copy in copies:
        copy.wait()


def any_space(count):
    return [pl.BlockSpec(memory_space=pltpu.HBM)] * count


def forward(hidden, weight):
    return pl.pallas_call(
        forward_kernel,
        in_specs=vmem(2),
        out_specs=pl.BlockSpec(memory_space=pltpu.VMEM),
        out_shape=jax.ShapeDtypeStruct((ROWS, D), BF16),
        scratch_shapes=[pltpu.VMEM((ROWS, FF), BF16), pltpu.VMEM((ROWS, D), F32)],
        compiler_params=params(24),
        cost_estimate=pl.CostEstimate(
            flops=2 * ROWS * FF * D, bytes_accessed=2 * (FF * D + ROWS * FF), transcendentals=ROWS * FF
        ),
        name="owner_forward",
    )(hidden, weight)


def pack(counts, branch):
    return pl.pallas_call(
        pack_kernel,
        in_specs=vmem(2),
        out_specs=pl.BlockSpec(memory_space=pltpu.HBM),
        scratch_shapes=[pltpu.VMEM((BLK, MSG, LANES), BF16), pltpu.SemaphoreType.DMA((PARTS,))],
        out_shape=pltpu.HBM((BLK, MSG, LANES), BF16),
        compiler_params=params(16),
        cost_estimate=pl.CostEstimate(
            flops=3 * 10**9, bytes_accessed=2**12, transcendentals=0
        ),
        name="owner_pack",
    )(counts, branch)


def texts_kernel(near_ref, first_ref, second_ref, third_ref, texts_ref):
    height = STEPS * IMAGES
    for at, ref in enumerate((near_ref, first_ref, second_ref, third_ref)):
        text = ref[...].astype(F32)
        norm = jnp.sqrt(jnp.sum(text * text, axis=1, keepdims=True) + 1e-06)
        texts_ref[at * height : (at + 1) * height, :] = (text / norm).astype(BF16)


def normalised(ring):
    return pl.pallas_call(
        texts_kernel,
        in_specs=vmem(4),
        out_specs=pl.BlockSpec(memory_space=pltpu.VMEM),
        out_shape=pltpu.HBM((STEPS * STEPS * IMAGES, D), BF16),
        compiler_params=params(12),
        cost_estimate=pl.CostEstimate(flops=1, bytes_accessed=2**20, transcendentals=0),
        name="normalise_texts",
    )(*ring)


def prepare_kernel(
    owners_row_ref, owners_col_ref, sizes_row_ref, sizes_col_ref, counts_ref, labels_ref, columns_ref,
    to_slots_ref, to_message_ref, to_rows_ref, facts_ref, member3_ref,
):
    owners = owners_col_ref[...]
    hits = owners == iota((SLOTS, BLK), 1)
    earlier = (iota((SLOTS, SLOTS), 0) > iota((SLOTS, SLOTS), 1)).astype(F32).astype(BF16)
    prefix = jnp.dot(earlier, hits.astype(F32).astype(BF16), preferred_element_type=F32)
    rank = jnp.sum(jnp.where(hits, prefix, 0.0), axis=1, keepdims=True).astype(I32)
    place = jnp.where(rank < CAP, owners * CAP + rank, WIDE + owners)
    place = jnp.where(owners >= 0, place, -1)
    to_slots_ref[...] = (iota((SLOTS, SLOT_K), 1) == place).astype(F32).astype(BF16)

    owners = owners_row_ref[...]
    hits = owners == iota((BLK, SLOTS), 0)
    earlier = (iota((SLOTS, SLOTS), 0) < iota((SLOTS, SLOTS), 1)).astype(F32).astype(BF16)
    prefix = jnp.dot(hits.astype(F32).astype(BF16), earlier, preferred_element_type=F32)
    rank = jnp.sum(jnp.where(hits, prefix, 0.0), axis=0, keepdims=True).astype(I32)
    place = jnp.where(rank < CAP, owners * CAP + rank, WIDE + owners)
    place = jnp.where(owners >= 0, place, -1)
    to_message_ref[...] = (iota((WIDE + BLK, SLOTS), 0) == place).astype(F32).astype(BF16)

    counts = counts_ref[...].astype(F32)
    starts = starts_of(counts)
    own = iota((BLK, SLOT_K), 0)
    lane = iota((BLK, SLOT_K), 1)
    extra = lane >= WIDE
    mine = jnp.where(extra, lane - WIDE, lane >> 4) == own
    rank = jnp.where(extra, CAP, lane & 15).astype(F32)
    valid = mine & (rank < counts[:, :1])
    key = jnp.sum(jnp.where(valid, starts[:, :1] + rank + 1.0, 0.0), axis=0, keepdims=True) - 1.0
    to_rows_ref[...] = (iota((ROWS, SLOT_K), 0).astype(F32) == key).astype(F32).astype(BF16)

    sizes_row = sizes_row_ref[...].astype(F32)
    sizes_col = sizes_col_ref[...].astype(F32)
    row = iota((IMAGES, IMAGES), 0)
    column = iota((IMAGES, IMAGES), 1)
    begin = jnp.sum(jnp.where(column < row, sizes_row, 0.0), axis=1, keepdims=True)
    slot = iota((IMAGES, SLOTS), 1).astype(F32)
    facts_ref[0:IMAGES, :] = ((slot >= begin) & (slot < begin + sizes_col)).astype(F32)
    facts_ref[IMAGES : 2 * IMAGES, :] = (labels_ref[...] == columns_ref[...]).astype(F32)
    facts_ref[2 * IMAGES :, :] = jnp.broadcast_to(sizes_col, (IMAGES, SLOTS))
    begin = jnp.sum(jnp.where(row < column, sizes_col, 0.0), axis=0, keepdims=True)
    slot = iota((SLOTS, IMAGES), 0).astype(F32)
    member = ((slot >= begin) & (slot < begin + sizes_row)).astype(F32)
    member3_ref[...] = jnp.concatenate([member, member, member], axis=1).astype(BF16)


def prepare(owners, patch_counts, counts, labels, columns):
    shapes = (
        (SLOTS, SLOT_K), (WIDE + BLK, SLOTS), (ROWS, SLOT_K), (3 * IMAGES, SLOTS), (SLOTS, 3 * IMAGES),
    )
    return pl.pallas_call(
        prepare_kernel,
        in_specs=vmem(7),
        out_specs=vmem(5),
        out_shape=[pltpu.HBM(shape, F32 if at == 3 else BF16) for at, shape in enumerate(shapes)],
        compiler_params=params(24),
        cost_estimate=pl.CostEstimate(flops=100*10**9, bytes_accessed=2**12, transcendentals=0),
        name="prepare_onehots",
    )(owners[None, :], owners[:, None], patch_counts[None, :], patch_counts[:, None], counts,
      labels[:, None], columns[None, :])


def slot_kernel(
    arrived_ref, patch_hbm, half_hbm, other_hbm, to_slots_hbm, to_message_hbm, facts_hbm, member3_hbm, weight_hbm,
    patches_hbm, send_ref, weight_ref,
    patch_ref, texts_ref, to_slots_ref, to_message_ref, facts_ref, member3_ref,
    patches_ref, rows_ref, summed, normed_low, scale_ref, spread_ref, sems,
):
    moves = [
        pltpu.make_async_copy(source, target, sems.at[at])
        for at, (source, target) in enumerate((
            (to_slots_hbm, to_slots_ref), (patch_hbm, patch_ref),
            (facts_hbm, facts_ref), (half_hbm, texts_ref.at[: SLOTS // 2, :]),
            (other_hbm, texts_ref.at[SLOTS // 2 :, :]),
            (member3_hbm, member3_ref), (to_message_hbm, to_message_ref),
        ))
    ]
    for copy in moves:
        copy.start()
    take_message(arrived_ref, rows_ref)
    moves[0].wait()
    to_slots = to_slots_ref[...]
    width = 512
    for part in range(D // width):
        columns = slice(part * width, (part + 1) * width)
        summed[:, columns] = jnp.dot(to_slots, rows_ref[:, columns], preferred_element_type=F32)

    height = 128
    moves[1].wait()
    weight_copy = pltpu.make_async_copy(weight_hbm, weight_ref, sems.at[8])
    weight_copy.start()

    for at in range(SLOTS // height):
        rows = pl.ds(at * height, height)
        values = summed[rows, :] + patch_ref[rows, :].astype(F32)
        centered = values - jnp.sum(values, axis=1, keepdims=True) * (1.0 / D)
        variance = jnp.sum(centered * centered, axis=1, keepdims=True) * (1.0 / D)
        scale = lax.rsqrt(variance + 1e-06)
        normed = centered * scale
        summed[rows, :] = normed
        high = normed.astype(BF16)
        rows_ref[rows, :] = high
        normed_low[rows, :] = (normed - high.astype(F32)).astype(BF16)
        scale_ref[rows, :] = jnp.broadcast_to(scale, (height, LANES))

    moves[2].wait()
    member = facts_ref[0:IMAGES, :].astype(BF16)
    sizes = facts_ref[2 * IMAGES :, :][:, :1]
    pooled = jnp.dot(member, rows_ref[0:SLOTS, :], preferred_element_type=F32)
    pooled = pooled + jnp.dot(member, normed_low[...], preferred_element_type=F32)
    pooled = pooled / sizes
    embed_norm = jnp.sqrt(jnp.sum(pooled * pooled, axis=1, keepdims=True) + 1e-06)
    embedding = pooled / embed_norm
    embed_b = embedding.astype(BF16)
    moves[3].wait()
    moves[4].wait()
    texts = texts_ref[...]
    logits = LOGIT_SCALE_TEMP * lax.dot_general(
        embed_b, texts, (((1,), (1,)), ((), ())), preferred_element_type=F32
    ) + LOGIT_BIAS_SHIFT
    positive = facts_ref[IMAGES : 2 * IMAGES, :]
    sigmoid = 1.0 / (1.0 + jnp.exp(-logits))
    weights = (LOSS_SCALE_FACTOR * LOGIT_SCALE_TEMP * (sigmoid - positive)).astype(BF16)
    embed_grad = jnp.dot(weights, texts, preferred_element_type=F32)
    radial = jnp.sum(embedding * embed_grad, axis=1, keepdims=True)
    spread = (embed_grad - embedding * radial) / embed_norm / sizes
    spread = spread - jnp.sum(spread, axis=1, keepdims=True) * (1.0 / D)
    for piece in range(3):
        top = spread.astype(BF16)
        spread_ref[piece * IMAGES : (piece + 1) * IMAGES, :] = top
        spread = spread - top.astype(F32)

    moves[5].wait()

    for at in range(SLOTS // height):
        rows = pl.ds(at * height, height)
        grad = jnp.dot(member3_ref[rows, :], spread_ref[...], preferred_element_type=F32)
        normed = summed[rows, :]
        mean_cross = jnp.sum(grad * normed, axis=1, keepdims=True) * (1.0 / D)
        scale = scale_ref[rows, :][:, :1]
        patches_ref[rows, :] = ((grad - normed * mean_cross) * scale).astype(BF16)

    out = pltpu.make_async_copy(patches_ref, patches_hbm, sems.at[7])
    out.start()
    moves[6].wait()
    put_extra(send_ref, jnp.dot(to_message_ref[WIDE:, :], patches_ref[...], preferred_element_type=F32))
    for part in range(PARTS):
        wide = jnp.dot(
            to_message_ref[:WIDE, :], patches_ref[:, part * PART : (part + 1) * PART],
            preferred_element_type=F32,
        )
        put_rows(send_ref, part, wide.astype(BF16))
    out.wait()
    weight_copy.wait()


def slots(arrived, patch_input, half, other, to_slots, to_message, facts, member3, weight):
    return pl.pallas_call(
        slot_kernel,
        in_specs=vmem(1) + any_space(8),
        out_specs=any_space(1) + vmem(2),
        out_shape=[
            jax.ShapeDtypeStruct((SLOTS, D), BF16),
            jax.ShapeDtypeStruct((BLK, MSG, LANES), BF16),
            pltpu.VMEM((FF, D), BF16),
        ],
        scratch_shapes=[
            pltpu.VMEM((SLOTS, D), BF16),
            pltpu.VMEM((SLOTS, D), BF16),
            pltpu.VMEM((SLOTS, SLOT_K), BF16),
            pltpu.VMEM((WIDE + BLK, SLOTS), BF16),
            pltpu.VMEM((3 * IMAGES, SLOTS), F32),
            pltpu.VMEM((SLOTS, 3 * IMAGES), BF16),
            pltpu.VMEM((SLOTS, D), BF16),
            pltpu.VMEM((SLOT_K, D), BF16),
            pltpu.VMEM((SLOTS, D), F32),
            pltpu.VMEM((SLOTS, D), BF16),
            pltpu.VMEM((SLOTS, LANES), F32),
            pltpu.VMEM((3 * IMAGES, D), BF16),
            pltpu.SemaphoreType.DMA((9,)),
        ],
        compiler_params=params(28),
        cost_estimate=pl.CostEstimate(
            flops=4 * SLOTS * SLOT_K * D, bytes_accessed=10 * 2**20, transcendentals=IMAGES * SLOTS
        ),
        name="slot_gradients",
    )(arrived, *(pltpu.with_memory_space_constraint(a, pltpu.HBM) for a in (
        patch_input, half, other, to_slots, to_message, facts, member3, weight
    )))


def slope(entries):
    square = entries * entries
    half = 0.5 * jnp.tanh(entries * (GELU_A + GELU_A * GELU_B * square)) + 0.5
    rise = entries * (2.0 * GELU_A + 6.0 * GELU_A * GELU_B * square)
    return half + half * (1.0 - half) * rise


def backward_kernel(
    arrived_ref, to_rows_ref, hidden_ref, weight_ref, out_ref, out_buf, rows_ref, sems
):
    take_message(arrived_ref, rows_ref)
    grads = jnp.dot(to_rows_ref[...], rows_ref[...], preferred_element_type=F32).astype(BF16)
    rows_ref[0:ROWS, :] = grads
    copies = []
    for k in range(CHUNKS):
        part = slice(k * CHUNK, (k + 1) * CHUNK)
        active_grad = lax.dot_general(
            rows_ref[0:ROWS, :], weight_ref[part, :], (((1,), (1,)), ((), ())),
            preferred_element_type=F32,
        )
        out_buf[:, part] = (slope(hidden_ref[:, part].astype(F32)) * active_grad).astype(BF16)
        copy = pltpu.make_async_copy(out_buf.at[:, part], out_ref.at[:, part], sems.at[k])
        copy.start()
        copies.append(copy)
    for copy in copies:
        copy.wait()


def backward(arrived, to_rows, hidden, weight):
    return pl.pallas_call(
        backward_kernel,
        in_specs=vmem(4),
        out_specs=pl.BlockSpec(memory_space=pl.ANY),
        out_shape=jax.ShapeDtypeStruct((ROWS, FF), BF16),
        scratch_shapes=[
            pltpu.VMEM((ROWS, FF), BF16),
            pltpu.VMEM((SLOT_K, D), BF16),
            pltpu.SemaphoreType.DMA((CHUNKS,)),
        ],
        compiler_params=params(26),
        cost_estimate=pl.CostEstimate(
            flops=2 * ROWS * FF * D, bytes_accessed=2 * (FF * D + 2 * ROWS * FF), transcendentals=ROWS * FF
        ),
        name="owner_backward",
    )(arrived, to_rows, hidden, weight)


def on_device(
    patch_input, hidden_pre, down_weight, text_features, patch_counts, owners, pair_labels
):
    position = lax.axis_index("blk")
    place = lax.axis_index("grp")
    grp_count = lax.axis_size("grp")
    tallies = tally(owners)
    text, tallies = lax.optimization_barrier((text_features, tallies))
    met = [text]
    for distance in range(1, STEPS):
        route = [((i - distance) % BLK, i) for i in range(BLK)]
        met.append(lax.ppermute(text, "blk", route))
    branch = forward(hidden_pre, down_weight)
    branch, position, place, *met = lax.optimization_barrier((branch, position, place, *met))
    near = jnp.concatenate(met, axis=0)
    near, tallies = lax.optimization_barrier((near, tallies))

    def swapped(block, masks):
        return lax.ppermute(block, "grp", [(i, i ^ masks[i % 2]) for i in range(grp_count)])

    first = swapped(near, (6, 2))
    counts = lax.all_to_all(tallies, "blk", split_axis=0, concat_axis=0, tiled=True)
    third = swapped(first, (2, 6))
    near_again, first = lax.optimization_barrier((near, first))
    second = swapped(near_again, (2, 6))
    message = pack(counts, branch)
    message, owners, patch_counts, pair_labels, near, first = lax.optimization_barrier(
        (message, owners, patch_counts, pair_labels, near, first)
    )
    ring = (near, first, second, third)
    arrived = lax.all_to_all(message, "blk", split_axis=0, concat_axis=0, tiled=True)

    half = normalised(ring)
    other = lax.ppermute(half, "grp", [(i, i ^ 1) for i in range(grp_count)])
    at = jnp.arange(grp_count * STEPS * IMAGES, dtype=I32)
    source = (position - (at // IMAGES) % STEPS) % BLK
    hop = at // (STEPS * IMAGES) % STEPS
    holder = jnp.where(at < STEPS * STEPS * IMAGES, place, place ^ 1)
    near_mask = jnp.where(holder % 2 == 0, 6, 2)
    mask = jnp.where(hop == 1, near_mask, jnp.where(hop == 2, 8 - near_mask, 4 * (hop // 3)))
    device = holder ^ mask
    columns = source * (grp_count * IMAGES) + device * IMAGES + at % IMAGES

    to_slots, to_message, to_rows, facts, member3 = prepare(
        owners, patch_counts, counts, pair_labels, columns
    )
    d_patches, outgoing, weight_near = slots(
        arrived, patch_input, half, other, to_slots, to_message, facts, member3, down_weight
    )
    returned = lax.all_to_all(outgoing, "blk", split_axis=0, concat_axis=0, tiled=True)
    d_hidden = backward(returned, to_rows, hidden_pre, weight_near)
    return (d_patches, d_hidden)


def solution(mesh):
    rows = P(("blk", "grp"), None)
    flat = P(("blk", "grp"))
    return jax.shard_map(
        on_device,
        mesh=mesh,
        in_specs=(rows, rows, P(), rows, flat, flat, flat),
        out_specs=(rows, rows),
        check_vma=False,
    )
```

```python
import jax
import jax.numpy as jnp
from jax import lax
from jax.experimental import pallas as pl
from jax.experimental.pallas import tpu as pltpu
from jax.sharding import PartitionSpec as P

STEPS = 4
GELU_A = 0.7978845608028654
GELU_B = 0.044715
LOGIT_SCALE_TEMP = 10.0
LOGIT_BIAS_SHIFT = -2.0
LOSS_SCALE_FACTOR = 128.0

BLK = 32
CAP = 16
D = 1536
FF = 3072
SLOTS = 512
ROWS = 288
IMAGES = 16
LANES = 128
TILES = D // LANES
MSG = (TILES + 1) * CAP
WIDE = BLK * CAP
CHUNK = 512
CHUNKS = FF // CHUNK
PART = 512
PARTS = D // PART
SLOT_K = 640
F32 = jnp.float32
BF16 = jnp.bfloat16
I32 = jnp.int32


def iota(shape, axis):
    return lax.broadcasted_iota(I32, shape, axis)


def vmem(count):
    return [pl.BlockSpec(memory_space=pltpu.VMEM)] * count


def params(mib):
    return pltpu.CompilerParams(vmem_limit_bytes=mib * 2**20)


def put_rows(send_ref, part, wide):
    for tile in range(PART // LANES):
        start = (part * (PART // LANES) + tile) * CAP
        send_ref[:, start : start + CAP, :] = wide[
            :, tile * LANES : (tile + 1) * LANES
        ].reshape(BLK, CAP, LANES)


def put_extra(send_ref, extra):
    last = extra.reshape(BLK, TILES, LANES)
    last = jnp.concatenate([last, jnp.zeros((BLK, CAP - TILES, LANES), F32)], axis=1)
    send_ref[:, TILES * CAP :, :] = last.astype(BF16)


def take_message(arrived_ref, rows_ref):
    for tile in range(TILES):
        rows_ref[0:WIDE, tile * LANES : (tile + 1) * LANES] = arrived_ref[
            :, tile * CAP : (tile + 1) * CAP, :
        ].reshape(WIDE, LANES)
    last = arrived_ref[:, TILES * CAP :, :].astype(F32)[:, :TILES, :]
    rows_ref[WIDE : WIDE + BLK, :] = last.reshape(BLK, D).astype(BF16)
    rows_ref[WIDE + BLK :, :] = jnp.zeros((SLOT_K - WIDE - BLK, D), BF16)


def starts_of(counts):
    before = (iota((BLK, BLK), 0) > iota((BLK, BLK), 1)).astype(F32).astype(BF16)
    return jnp.dot(before, counts.astype(BF16), preferred_element_type=F32)


def tally_kernel(owners_ref, tallies_ref):
    hits = (owners_ref[...] == iota((BLK, SLOTS), 0)).astype(I32)
    tallies_ref[...] = jnp.broadcast_to(jnp.sum(hits, axis=1, keepdims=True), (BLK, LANES))


def tally(owners):
    return pl.pallas_call(
        tally_kernel,
        in_specs=vmem(1),
        out_specs=pl.BlockSpec(memory_space=pltpu.VMEM),
        out_shape=jax.ShapeDtypeStruct((BLK, LANES), I32),
        compiler_params=params(2),
        cost_estimate=pl.CostEstimate(flops=10**10, bytes_accessed=2**15, transcendentals=0),
        name="tally_owners",
    )(pltpu.with_memory_space_constraint(owners[None, :], pltpu.HBM))


def gelu(entries):
    inside = GELU_A * (entries + GELU_B * entries * entries * entries)
    return 0.5 * entries * (1.0 + jnp.tanh(inside))


def forward_kernel(hidden_ref, weight_ref, branch_ref, active, total):
    hidden_buf, weight_buf = hidden_ref, weight_ref

    def activate(k):
        part = slice(k * CHUNK, (k + 1) * CHUNK)
        active[:, part] = gelu(hidden_buf[:, part].astype(F32)).astype(BF16)

    activate(0)
    for k in range(CHUNKS):
        if k + 1 < CHUNKS:
            activate(k + 1)
        part = slice(k * CHUNK, (k + 1) * CHUNK)
        product = jnp.dot(active[:, part], weight_buf[part, :], preferred_element_type=F32)
        if k == 0:
            total[...] = product
        else:
            total[...] += product

    branch_ref[...] = total[...].astype(BF16)


def pack_kernel(counts_ref, branch_ref, send_ref, buffer, sems):
    counts = counts_ref[...].astype(F32)
    starts = starts_of(counts)
    counts_wide = jnp.broadcast_to(counts[:, None, :], (BLK, CAP, LANES)).reshape(WIDE, LANES)[:, :1]
    starts_wide = jnp.broadcast_to(starts[:, None, :], (BLK, CAP, LANES)).reshape(WIDE, LANES)[:, :1]
    rank = (iota((WIDE, 1), 0) & 15).astype(F32)
    key = jnp.where(rank < counts_wide, starts_wide + rank, -1.0)
    pick = (iota((WIDE, ROWS), 1).astype(F32) == key).astype(F32).astype(BF16)
    extra_key = jnp.where(counts[:, :1] > CAP, starts[:, :1] + CAP, -1.0)
    extra_pick = (iota((BLK, ROWS), 1).astype(F32) == extra_key).astype(F32).astype(BF16)
    put_extra(buffer, jnp.dot(extra_pick, branch_ref[...], preferred_element_type=F32))
    copies = []
    begin = 0
    for part in range(PARTS):
        columns = slice(part * PART, (part + 1) * PART)
        wide = jnp.dot(pick, branch_ref[:, columns], preferred_element_type=F32).astype(BF16)
        put_rows(buffer, part, wide)
        end = (part + 1) * (PART // LANES) * CAP if part + 1 < PARTS else MSG
        copy = pltpu.make_async_copy(
            buffer.at[:, begin:end, :], send_ref.at[:, begin:end, :], sems.at[part]
        )
        copy.start()
        copies.append(copy)
        begin = end
    for copy in copies:
        copy.wait()


def any_space(count):
    return [pl.BlockSpec(memory_space=pltpu.HBM)] * count


def forward(hidden, weight):
    return pl.pallas_call(
        forward_kernel,
        in_specs=vmem(2),
        out_specs=pl.BlockSpec(memory_space=pltpu.VMEM),
        out_shape=jax.ShapeDtypeStruct((ROWS, D), BF16),
        scratch_shapes=[pltpu.VMEM((ROWS, FF), BF16), pltpu.VMEM((ROWS, D), F32)],
        compiler_params=params(24),
        cost_estimate=pl.CostEstimate(
            flops=2 * ROWS * FF * D, bytes_accessed=2 * (FF * D + ROWS * FF), transcendentals=ROWS * FF
        ),
        name="owner_forward",
    )(hidden, weight)


def pack(counts, branch):
    return pl.pallas_call(
        pack_kernel,
        in_specs=vmem(2),
        out_specs=pl.BlockSpec(memory_space=pltpu.HBM),
        scratch_shapes=[pltpu.VMEM((BLK, MSG, LANES), BF16), pltpu.SemaphoreType.DMA((PARTS,))],
        out_shape=pltpu.HBM((BLK, MSG, LANES), BF16),
        compiler_params=params(16),
        cost_estimate=pl.CostEstimate(
            flops=3 * 10**9, bytes_accessed=2**12, transcendentals=0
        ),
        name="owner_pack",
    )(counts, branch)


def texts_kernel(near_ref, first_ref, second_ref, third_ref, texts_ref):
    height = STEPS * IMAGES
    for at, ref in enumerate((near_ref, first_ref, second_ref, third_ref)):
        text = ref[...].astype(F32)
        norm = jnp.sqrt(jnp.sum(text * text, axis=1, keepdims=True) + 1e-06)
        texts_ref[at * height : (at + 1) * height, :] = (text / norm).astype(BF16)


def normalised(ring):
    return pl.pallas_call(
        texts_kernel,
        in_specs=vmem(4),
        out_specs=pl.BlockSpec(memory_space=pltpu.VMEM),
        out_shape=pltpu.HBM((STEPS * STEPS * IMAGES, D), BF16),
        compiler_params=params(12),
        cost_estimate=pl.CostEstimate(flops=1, bytes_accessed=2**20, transcendentals=0),
        name="normalise_texts",
    )(*ring)


def prepare_kernel(
    owners_row_ref, owners_col_ref, sizes_row_ref, sizes_col_ref, counts_ref, labels_ref, columns_ref,
    to_slots_ref, to_message_ref, to_rows_ref, facts_ref, member3_ref,
):
    owners = owners_col_ref[...]
    hits = owners == iota((SLOTS, BLK), 1)
    earlier = (iota((SLOTS, SLOTS), 0) > iota((SLOTS, SLOTS), 1)).astype(F32).astype(BF16)
    prefix = jnp.dot(earlier, hits.astype(F32).astype(BF16), preferred_element_type=F32)
    rank = jnp.sum(jnp.where(hits, prefix, 0.0), axis=1, keepdims=True).astype(I32)
    place = jnp.where(rank < CAP, owners * CAP + rank, WIDE + owners)
    place = jnp.where(owners >= 0, place, -1)
    to_slots_ref[...] = (iota((SLOTS, SLOT_K), 1) == place).astype(F32).astype(BF16)

    owners = owners_row_ref[...]
    hits = owners == iota((BLK, SLOTS), 0)
    earlier = (iota((SLOTS, SLOTS), 0) < iota((SLOTS, SLOTS), 1)).astype(F32).astype(BF16)
    prefix = jnp.dot(hits.astype(F32).astype(BF16), earlier, preferred_element_type=F32)
    rank = jnp.sum(jnp.where(hits, prefix, 0.0), axis=0, keepdims=True).astype(I32)
    place = jnp.where(rank < CAP, owners * CAP + rank, WIDE + owners)
    place = jnp.where(owners >= 0, place, -1)
    to_message_ref[...] = (iota((WIDE + BLK, SLOTS), 0) == place).astype(F32).astype(BF16)

    counts = counts_ref[...].astype(F32)
    starts = starts_of(counts)
    own = iota((BLK, SLOT_K), 0)
    lane = iota((BLK, SLOT_K), 1)
    extra = lane >= WIDE
    mine = jnp.where(extra, lane - WIDE, lane >> 4) == own
    rank = jnp.where(extra, CAP, lane & 15).astype(F32)
    valid = mine & (rank < counts[:, :1])
    key = jnp.sum(jnp.where(valid, starts[:, :1] + rank + 1.0, 0.0), axis=0, keepdims=True) - 1.0
    to_rows_ref[...] = (iota((ROWS, SLOT_K), 0).astype(F32) == key).astype(F32).astype(BF16)

    sizes_row = sizes_row_ref[...].astype(F32)
    sizes_col = sizes_col_ref[...].astype(F32)
    row = iota((IMAGES, IMAGES), 0)
    column = iota((IMAGES, IMAGES), 1)
    begin = jnp.sum(jnp.where(column < row, sizes_row, 0.0), axis=1, keepdims=True)
    slot = iota((IMAGES, SLOTS), 1).astype(F32)
    facts_ref[0:IMAGES, :] = ((slot >= begin) & (slot < begin + sizes_col)).astype(F32)
    facts_ref[IMAGES : 2 * IMAGES, :] = (labels_ref[...] == columns_ref[...]).astype(F32)
    facts_ref[2 * IMAGES :, :] = jnp.broadcast_to(sizes_col, (IMAGES, SLOTS))
    begin = jnp.sum(jnp.where(row < column, sizes_col, 0.0), axis=0, keepdims=True)
    slot = iota((SLOTS, IMAGES), 0).astype(F32)
    member = ((slot >= begin) & (slot < begin + sizes_row)).astype(F32)
    member3_ref[...] = jnp.concatenate([member, member, member], axis=1).astype(BF16)


def prepare(owners, patch_counts, counts, labels, columns):
    shapes = (
        (SLOTS, SLOT_K), (WIDE + BLK, SLOTS), (ROWS, SLOT_K), (3 * IMAGES, SLOTS), (SLOTS, 3 * IMAGES),
    )
    return pl.pallas_call(
        prepare_kernel,
        in_specs=vmem(7),
        out_specs=vmem(5),
        out_shape=[pltpu.HBM(shape, F32 if at == 3 else BF16) for at, shape in enumerate(shapes)],
        compiler_params=params(24),
        cost_estimate=pl.CostEstimate(flops=100*10**9, bytes_accessed=2**12, transcendentals=0),
        name="prepare_onehots",
    )(owners[None, :], owners[:, None], patch_counts[None, :], patch_counts[:, None], counts,
      labels[:, None], columns[None, :])


def slot_kernel(
    arrived_ref, patch_hbm, half_hbm, other_hbm, to_slots_hbm, to_message_hbm, facts_hbm, member3_hbm, weight_hbm,
    patches_hbm, send_ref, weight_ref,
    patch_ref, texts_ref, to_slots_ref, to_message_ref, facts_ref, member3_ref,
    patches_ref, rows_ref, summed, normed_low, scale_ref, spread_ref, sems,
):
    moves = [
        pltpu.make_async_copy(source, target, sems.at[at])
        for at, (source, target) in enumerate((
            (to_slots_hbm, to_slots_ref), (patch_hbm, patch_ref),
            (facts_hbm, facts_ref), (half_hbm, texts_ref.at[: SLOTS // 2, :]),
            (other_hbm, texts_ref.at[SLOTS // 2 :, :]),
            (member3_hbm, member3_ref), (to_message_hbm, to_message_ref),
        ))
    ]
    for copy in moves:
        copy.start()
    take_message(arrived_ref, rows_ref)
    moves[0].wait()
    to_slots = to_slots_ref[...]
    width = 512
    for part in range(D // width):
        columns = slice(part * width, (part + 1) * width)
        summed[:, columns] = jnp.dot(to_slots, rows_ref[:, columns], preferred_element_type=F32)

    height = 128
    moves[1].wait()
    weight_copy = pltpu.make_async_copy(weight_hbm, weight_ref, sems.at[8])
    weight_copy.start()

    for at in range(SLOTS // height):
        rows = pl.ds(at * height, height)
        values = summed[rows, :] + patch_ref[rows, :].astype(F32)
        centered = values - jnp.sum(values, axis=1, keepdims=True) * (1.0 / D)
        variance = jnp.sum(centered * centered, axis=1, keepdims=True) * (1.0 / D)
        scale = lax.rsqrt(variance + 1e-06)
        normed = centered * scale
        summed[rows, :] = normed
        high = normed.astype(BF16)
        rows_ref[rows, :] = high
        normed_low[rows, :] = (normed - high.astype(F32)).astype(BF16)
        scale_ref[rows, :] = jnp.broadcast_to(scale, (height, LANES))

    moves[2].wait()
    member = facts_ref[0:IMAGES, :].astype(BF16)
    sizes = facts_ref[2 * IMAGES :, :][:, :1]
    pooled = jnp.dot(member, rows_ref[0:SLOTS, :], preferred_element_type=F32)
    pooled = pooled + jnp.dot(member, normed_low[...], preferred_element_type=F32)
    pooled = pooled / sizes
    embed_norm = jnp.sqrt(jnp.sum(pooled * pooled, axis=1, keepdims=True) + 1e-06)
    embedding = pooled / embed_norm
    embed_b = embedding.astype(BF16)
    moves[3].wait()
    moves[4].wait()
    texts = texts_ref[...]
    logits = LOGIT_SCALE_TEMP * lax.dot_general(
        embed_b, texts, (((1,), (1,)), ((), ())), preferred_element_type=F32
    ) + LOGIT_BIAS_SHIFT
    positive = facts_ref[IMAGES : 2 * IMAGES, :]
    sigmoid = 1.0 / (1.0 + jnp.exp(-logits))
    weights = (LOSS_SCALE_FACTOR * LOGIT_SCALE_TEMP * (sigmoid - positive)).astype(BF16)
    embed_grad = jnp.dot(weights, texts, preferred_element_type=F32)
    radial = jnp.sum(embedding * embed_grad, axis=1, keepdims=True)
    spread = (embed_grad - embedding * radial) / embed_norm / sizes
    spread = spread - jnp.sum(spread, axis=1, keepdims=True) * (1.0 / D)
    for piece in range(3):
        top = spread.astype(BF16)
        spread_ref[piece * IMAGES : (piece + 1) * IMAGES, :] = top
        spread = spread - top.astype(F32)

    moves[5].wait()

    for at in range(SLOTS // height):
        rows = pl.ds(at * height, height)
        grad = jnp.dot(member3_ref[rows, :], spread_ref[...], preferred_element_type=F32)
        normed = summed[rows, :]
        mean_cross = jnp.sum(grad * normed, axis=1, keepdims=True) * (1.0 / D)
        scale = scale_ref[rows, :][:, :1]
        patches_ref[rows, :] = ((grad - normed * mean_cross) * scale).astype(BF16)

    out = pltpu.make_async_copy(patches_ref, patches_hbm, sems.at[7])
    out.start()
    moves[6].wait()
    put_extra(send_ref, jnp.dot(to_message_ref[WIDE:, :], patches_ref[...], preferred_element_type=F32))
    for part in range(PARTS):
        wide = jnp.dot(
            to_message_ref[:WIDE, :], patches_ref[:, part * PART : (part + 1) * PART],
            preferred_element_type=F32,
        )
        put_rows(send_ref, part, wide.astype(BF16))
    out.wait()
    weight_copy.wait()


def slots(arrived, patch_input, half, other, to_slots, to_message, facts, member3, weight):
    return pl.pallas_call(
        slot_kernel,
        in_specs=vmem(1) + any_space(8),
        out_specs=any_space(1) + vmem(2),
        out_shape=[
            jax.ShapeDtypeStruct((SLOTS, D), BF16),
            jax.ShapeDtypeStruct((BLK, MSG, LANES), BF16),
            pltpu.VMEM((FF, D), BF16),
        ],
        scratch_shapes=[
            pltpu.VMEM((SLOTS, D), BF16),
            pltpu.VMEM((SLOTS, D), BF16),
            pltpu.VMEM((SLOTS, SLOT_K), BF16),
            pltpu.VMEM((WIDE + BLK, SLOTS), BF16),
            pltpu.VMEM((3 * IMAGES, SLOTS), F32),
            pltpu.VMEM((SLOTS, 3 * IMAGES), BF16),
            pltpu.VMEM((SLOTS, D), BF16),
            pltpu.VMEM((SLOT_K, D), BF16),
            pltpu.VMEM((SLOTS, D), F32),
            pltpu.VMEM((SLOTS, D), BF16),
            pltpu.VMEM((SLOTS, LANES), F32),
            pltpu.VMEM((3 * IMAGES, D), BF16),
            pltpu.SemaphoreType.DMA((9,)),
        ],
        compiler_params=params(28),
        cost_estimate=pl.CostEstimate(
            flops=4 * SLOTS * SLOT_K * D, bytes_accessed=10 * 2**20, transcendentals=IMAGES * SLOTS
        ),
        name="slot_gradients",
    )(arrived, *(pltpu.with_memory_space_constraint(a, pltpu.HBM) for a in (
        patch_input, half, other, to_slots, to_message, facts, member3, weight
    )))


def slope(entries):
    square = entries * entries
    half = 0.5 * jnp.tanh(entries * (GELU_A + GELU_A * GELU_B * square)) + 0.5
    rise = entries * (2.0 * GELU_A + 6.0 * GELU_A * GELU_B * square)
    return half + half * (1.0 - half) * rise


def backward_kernel(
    arrived_ref, to_rows_ref, hidden_ref, weight_ref, out_ref, out_buf, rows_ref, sems
):
    take_message(arrived_ref, rows_ref)
    grads = jnp.dot(to_rows_ref[...], rows_ref[...], preferred_element_type=F32).astype(BF16)
    rows_ref[0:ROWS, :] = grads
    copies = []
    for k in range(CHUNKS):
        part = slice(k * CHUNK, (k + 1) * CHUNK)
        active_grad = lax.dot_general(
            rows_ref[0:ROWS, :], weight_ref[part, :], (((1,), (1,)), ((), ())),
            preferred_element_type=F32,
        )
        out_buf[:, part] = (slope(hidden_ref[:, part].astype(F32)) * active_grad).astype(BF16)
        copy = pltpu.make_async_copy(out_buf.at[:, part], out_ref.at[:, part], sems.at[k])
        copy.start()
        copies.append(copy)
    for copy in copies:
        copy.wait()


def backward(arrived, to_rows, hidden, weight):
    return pl.pallas_call(
        backward_kernel,
        in_specs=vmem(4),
        out_specs=pl.BlockSpec(memory_space=pl.ANY),
        out_shape=jax.ShapeDtypeStruct((ROWS, FF), BF16),
        scratch_shapes=[
            pltpu.VMEM((ROWS, FF), BF16),
            pltpu.VMEM((SLOT_K, D), BF16),
            pltpu.SemaphoreType.DMA((CHUNKS,)),
        ],
        compiler_params=params(26),
        cost_estimate=pl.CostEstimate(
            flops=2 * ROWS * FF * D, bytes_accessed=2 * (FF * D + 2 * ROWS * FF), transcendentals=ROWS * FF
        ),
        name="owner_backward",
    )(arrived, to_rows, hidden, weight)


def on_device(
    patch_input, hidden_pre, down_weight, text_features, patch_counts, owners, pair_labels
):
    position = lax.axis_index("blk")
    place = lax.axis_index("grp")
    grp_count = lax.axis_size("grp")
    tallies = tally(owners)
    text, tallies = lax.optimization_barrier((text_features, tallies))
    met = [text]
    for distance in range(STEPS - 1, 0, -1):
        route = [((i - distance) % BLK, i) for i in range(BLK)]
        met.insert(1, lax.ppermute(text, "blk", route))
    branch = forward(hidden_pre, down_weight)
    branch, position, place, *met = lax.optimization_barrier((branch, position, place, *met))
    near = jnp.concatenate(met, axis=0)
    near, tallies = lax.optimization_barrier((near, tallies))

    def swapped(block, masks):
        return lax.ppermute(block, "grp", [(i, i ^ masks[i % 2]) for i in range(grp_count)])

    first = swapped(near, (6, 2))
    counts = lax.all_to_all(tallies, "blk", split_axis=0, concat_axis=0, tiled=True)
    third = swapped(first, (2, 6))
    near_again, first = lax.optimization_barrier((near, first))
    second = swapped(near_again, (2, 6))
    message = pack(counts, branch)
    message, owners, patch_counts, pair_labels, near, first = lax.optimization_barrier(
        (message, owners, patch_counts, pair_labels, near, first)
    )
    ring = (near, first, second, third)
    arrived = lax.all_to_all(message, "blk", split_axis=0, concat_axis=0, tiled=True)

    half = normalised(ring)
    other = lax.ppermute(half, "grp", [(i, i ^ 1) for i in range(grp_count)])
    at = jnp.arange(grp_count * STEPS * IMAGES, dtype=I32)
    source = (position - (at // IMAGES) % STEPS) % BLK
    hop = at // (STEPS * IMAGES) % STEPS
    holder = jnp.where(at < STEPS * STEPS * IMAGES, place, place ^ 1)
    near_mask = jnp.where(holder % 2 == 0, 6, 2)
    mask = jnp.where(hop == 1, near_mask, jnp.where(hop == 2, 8 - near_mask, 4 * (hop // 3)))
    device = holder ^ mask
    columns = source * (grp_count * IMAGES) + device * IMAGES + at % IMAGES

    to_slots, to_message, to_rows, facts, member3 = prepare(
        owners, patch_counts, counts, pair_labels, columns
    )
    d_patches, outgoing, weight_near = slots(
        arrived, patch_input, half, other, to_slots, to_message, facts, member3, down_weight
    )
    returned = lax.all_to_all(outgoing, "blk", split_axis=0, concat_axis=0, tiled=True)
    d_hidden = backward(returned, to_rows, hidden_pre, weight_near)
    return (d_patches, d_hidden)


def solution(mesh):
    rows = P(("blk", "grp"), None)
    flat = P(("blk", "grp"))
    return jax.shard_map(
        on_device,
        mesh=mesh,
        in_specs=(rows, rows, P(), rows, flat, flat, flat),
        out_specs=(rows, rows),
        check_vma=False,
    )
```
